32 devices in a mesh: seg: 8 (over z, x), col: 4 (over y, core).
Axes of the slice: x: 2, y: 2, z: 4, core: 2. Of those that a mesh axis runs over, the one named last changes fastest.
Arguments:
- margin: float32 [1536, 1536], P('seg'), as said below
- leaf_factor: float32 [1536, 1536], P('seg', 'col'), as said below
Outputs:
- factor: float32 [1536, 1536], P('seg', 'col')
- errors: float32 [2], replicated
Inputs may be any that keep to these rules, and one draw needn't show every extreme that they name: margin is symmetric and positive definite; entries with |row - column| >= 2048 are zero. leaf_factor is zero outside the four diagonal blocks of 384 rows and columns; each block is upper triangular.
All inputs are finite; a program needn't handle non-finite values.
Results may differ from the reference program's by a relative error of at most 0.00005.
Values sent between devices are 32-bit elements; how exact they have to be, the bound alone decides.
A program may use at most 64 MiB of HBM per device.

```python
import jax
import jax.numpy as jnp
from jax import lax

BAND = 2048
N = 1536


def margin_parts(key):
    base_key = jax.random.fold_in(key, 7)
    entry_key, rough_key, diag_key, noise_key = jax.random.split(base_key, 4)
    indices = jnp.arange(N)
    distance = indices[:, None] - indices[None, :]
    inband = (distance >= 0) & (distance < BAND)
    entries = jax.random.normal(entry_key, (N, N), jnp.float32)
    diagonal = jax.random.uniform(diag_key, (N,), jnp.float32, 0.5, 1.5)
    rough = jax.random.uniform(rough_key, (N,), jnp.float32, 0.7, 1.3)
    rising = 0.6 + 0.6 * indices.astype(jnp.float32) / N
    sigma = 0.5 / jnp.sqrt(jnp.float32(BAND))
    lower = jnp.where(inband, entries, 0.0) * (sigma * rough * rising)[:, None]
    margin = jnp.dot(lower, lower.T, precision=lax.Precision.HIGHEST) + jnp.diag(diagonal)
    margin = 0.5 * (margin + margin.T)
    return (margin, noise_key)


def draw_margin(key, part):
    margin, noise_key = margin_parts(key)
    return margin


def draw_leaf_factor(key, part):
    margin, noise_key = margin_parts(key)
    quarter = N // 4
    identity = jnp.eye(quarter, dtype=jnp.float32)
    upper_mask = jnp.arange(quarter)[:, None] <= jnp.arange(quarter)[None, :]
    blocks = []
    for quarter_idx in range(4):
        lo_edge = quarter_idx * quarter
        diag_block = margin[lo_edge:lo_edge + quarter, lo_edge:lo_edge + quarter]
        lower_chol = jnp.linalg.cholesky(diag_block)
        inverse = jax.scipy.linalg.solve_triangular(lower_chol, identity, lower=True)
        noise = jax.random.normal(jax.random.fold_in(noise_key, quarter_idx), (quarter, quarter), jnp.float32)
        perturb = jnp.where(upper_mask, noise, 0.0) * (0.2 / jnp.sqrt(jnp.float32(quarter)))
        blocks.append(inverse.T + perturb)
    return jax.scipy.linalg.block_diag(*blocks)


def setup_inputs(seed: int = 0) -> dict:
    streams_of = jax.random.split(jax.random.key(seed), 3)
    margin = draw_margin(jax.random.fold_in(streams_of[2], 71), 0)
    leaf_factor = draw_leaf_factor(jax.random.fold_in(streams_of[2], 71), 0)
    return {"margin": margin, "leaf_factor": leaf_factor}


def matmul(left, right):
    return jnp.dot(left.astype(jnp.float32), right.astype(jnp.float32), precision=lax.Precision.HIGHEST, preferred_element_type=jnp.float32)

def refine(margin, factor):
    applied = matmul(margin, factor)
    coupling = matmul(factor.T, applied)
    defect = jnp.eye(N, dtype=jnp.float32) - coupling
    squares = jnp.sum(defect * defect)
    return (factor + 0.5 * matmul(factor, defect), squares)

def reference(margin, leaf_factor):
    halves = jnp.arange(N) // (N // 2)
    split_margin = jnp.where(halves[:, None] == halves[None, :], margin, jnp.float32(0.0))
    middle, squares_low = refine(split_margin, leaf_factor)
    factor, squares_top = refine(margin, middle)
    errors = jnp.sqrt(jnp.stack([squares_low, squares_top]) / N)
    return (factor, errors)
```

```python
import functools

import jax
import jax.numpy as jnp
from jax import lax
from jax.experimental import pallas as pl
from jax.experimental.pallas import tpu as pltpu
from jax.sharding import PartitionSpec as P

MESH = pl.DeviceIdType.MESH
F32 = jnp.float32
CHUNKS = 3
SENDS = 128


def dot(left, right, left_dim=1):
    return lax.dot_general(
        left,
        right,
        (((left_dim,), (0,)), ((), ())),
        precision=lax.Precision.HIGHEST,
        preferred_element_type=F32,
    )


def fold(values):
    rows, width = values.shape
    tall = jnp.sum(values.reshape(rows // 8, 8, width), axis=0)
    total = tall[:, :128]
    for start in range(128, width, 128):
        total = total + tall[:, start:start + 128]
    return total


def kernel(
    nseg, ncol, order,
    margin_ref, leaf_ref, out_ref, err_ref,
    sblk, lcol, lrow, part, rk, kcol, rp, rm, mb, eb, jb, sq1, sq2,
    send, lz_r, lx_r, lrow_r, rk_r, kz_r, kx_r, row_r, pair_r, m_r, e_r, q1_r, q2_r, local,
):
    rows, width = leaf_ref.shape
    nx = nseg // 4
    cq = ncol // 4
    hs, hc = nseg // 2, ncol // 2
    per = width // rows
    quarter = nx * rows
    step = rows // CHUNKS

    seg = lax.axis_index("seg")
    col = lax.axis_index("col")
    z, x = lax.div(seg, nx), lax.rem(seg, nx)
    qc = lax.div(col, cq)
    hseg, hcol = lax.div(z, 2), lax.div(qc, 2)
    diag = hseg == hcol
    mine = lax.rem(col, hc)
    half_col = col - mine

    pending = []
    used = [0]

    def true():
        return seg >= 0

    def push(cond, src, dst, rsem, to_seg, to_col):
        index = used[0]
        used[0] += 1
        copy = pltpu.make_async_remote_copy(
            src_ref=src, dst_ref=dst, send_sem=send.at[index], recv_sem=rsem,
            device_id=(to_seg, to_col), device_id_type=MESH,
        )
        if cond is None:
            copy.start()
        else:
            pl.when(cond)(copy.start)
        pending.append((cond, copy))

    def arrive(cond, dst, rsem):
        copy = pltpu.make_async_remote_copy(
            src_ref=dst, dst_ref=dst, send_sem=send.at[0], recv_sem=rsem,
            device_id=(seg, lax.rem(col + 1, ncol)), device_id_type=MESH,
        )
        if cond is None:
            copy.wait_recv()
        else:
            pl.when(cond)(copy.wait_recv)

    def other_x(d):
        return z * nx + lax.rem(x + d, nx)

    fetch = pltpu.make_async_copy(
        margin_ref.at[:, pl.ds(pl.multiple_of(qc * quarter, 128), quarter)], sblk, local.at[0]
    )
    fetch.start()
    owner = qc == z
    own_slot = lax.rem(col, cq)

    @pl.when(owner)
    def _():
        lcol[x] = leaf_ref[...]
        lrow[own_slot] = leaf_ref[...]

    barrier = pltpu.get_barrier_semaphore()
    for d in range(1, nseg):
        pl.semaphore_signal(barrier, inc=1, device_id=(lax.rem(seg + d, nseg), col), device_id_type=MESH)
    for d in range(1, ncol):
        pl.semaphore_signal(barrier, inc=1, device_id=(seg, lax.rem(col + d, ncol)), device_id_type=MESH)
    pl.semaphore_wait(barrier, nseg + ncol - 2)

    for j in range(CHUNKS):
        here = pl.ds(j * step, step)
        block = lcol.at[x, here]
        arrive(jnp.logical_not(owner), block, lz_r.at[j])
        push((z >= qc) & (z < 3), block, block, lz_r.at[j], seg + nx, col)
        push((z <= qc) & (z > 0), block, block, lz_r.at[j], seg - nx, col)
        for d in range(1, nx):
            push(None, block, block, lx_r.at[x, j], other_x(d), col)
    for d in range(1, ncol):
        push(owner, lrow.at[own_slot], lrow.at[own_slot], lrow_r.at[own_slot], seg, lax.rem(col + d, ncol))
    for d in range(1, nx):
        from_x = lax.rem(x + d, nx)
        for j in range(CHUNKS):
            arrive(None, lcol.at[from_x, pl.ds(j * step, step)], lx_r.at[from_x, j])
    fetch.wait()
    applied = dot(sblk[...], lcol[...].reshape(quarter, width))
    for k in range(cq):
        arrive(jnp.logical_not(owner & (own_slot == k)), lrow.at[k], lrow_r.at[k])
    for k in range(cq):
        piece = dot(lrow[k], applied, 0)
        part[pl.ds(k * per, per)] = piece.reshape(per, rows, width)
    for d in range(1, nx):
        push(None, part.at[lax.rem(x + d, nx)], rk.at[x], rk_r.at[x], other_x(d), col)
    total = part[x]
    for d in range(1, nx):
        from_x = lax.rem(x + d, nx)
        arrive(None, rk.at[from_x], rk_r.at[from_x])
        total = total + rk[from_x]
    kcol[seg] = total

    def spread(distance, up):
        origin = z - distance if up else z + distance
        valid = (origin >= 0) & (origin <= 3)
        wide = lax.div(origin, 2) == hcol
        same = lax.div(origin, 2) == hseg
        reached = valid & (wide | same)
        low = jnp.where(wide, 0, 2 * hseg)
        high = jnp.where(wide, 3, 2 * hseg + 1)
        slot = jnp.clip(origin, 0, 3) * nx + x
        plane = jnp.clip(origin, 0, 3)
        for j in range(CHUNKS):
            block = kcol.at[slot, pl.ds(j * step, step)]
            if distance:
                arrive(reached, block, kz_r.at[plane, j])
            if up or distance == 0:
                push(reached & (z < high), block, block, kz_r.at[plane, j], seg + nx, col)
            if not up or distance == 0:
                push(reached & (z > low), block, block, kz_r.at[plane, j], seg - nx, col)
            for d in range(1, nx):
                push(reached, block, block, kx_r.at[slot, j], other_x(d), col)

    def settle(distance, up):
        origin = z - distance if up else z + distance
        valid = (origin >= 0) & (origin <= 3)
        reached = valid & ((lax.div(origin, 2) == hcol) | (lax.div(origin, 2) == hseg))
        for d in range(1, nx):
            slot = jnp.clip(origin, 0, 3) * nx + lax.rem(x + d, nx)
            for j in range(CHUNKS):
                arrive(reached, kcol.at[slot, pl.ds(j * step, step)], kx_r.at[slot, j])

    spread(0, False)

    partner = lax.rem(col + hc, ncol)
    row_ids = seg * rows + lax.broadcasted_iota(jnp.int32, (rows, width), 0)
    col_ids = col * width + lax.broadcasted_iota(jnp.int32, (rows, width), 1)
    identity = (row_ids == col_ids).astype(F32)

    def siblings(cond, buf, rsem, which):
        for d in range(1, hc):
            push(cond, buf.at[mine], buf.at[mine], rsem.at[which, mine], seg, half_col + lax.rem(mine + d, hc))

    def from_siblings(cond, buf, rsem, which):
        for d in range(1, hc):
            k = lax.rem(mine + d, hc)
            arrive(cond, buf.at[k], rsem.at[which, k])

    @pl.when(diag)
    def _():
        own = kcol[seg]
        defect = identity - own
        sq1[seg, pl.ds(0, 8)] = fold(defect * defect)
        rp[mine] = 1.5 * identity - 0.5 * own

    @pl.when(jnp.logical_not(diag))
    def _():
        sq1[seg, pl.ds(0, 8)] = jnp.zeros((8, 128), F32)

    push(diag, rp.at[mine], rp.at[mine], pair_r.at[0], seg, partner)
    siblings(diag, rp, row_r, 0)

    spread(1, True)
    spread(1, False)
    spread(2, True)
    spread(2, False)
    spread(3, True)
    spread(3, False)
    off = jnp.logical_not(diag)
    arrive(off, rp.at[mine], pair_r.at[0])
    siblings(off, rp, row_r, 0)

    settle(0, False)

    @pl.when(diag)
    def _():
        near = kcol[pl.ds(z * nx, nx)].reshape(quarter, width)
        update = jnp.zeros((rows, width), F32)
        for k in range(cq):
            update = update + dot(lrow[k], near[k * width:(k + 1) * width])
        mb[mine] = 1.5 * leaf_ref[...] - 0.5 * update

    siblings(diag, mb, m_r, 0)
    settle(1, True)
    settle(1, False)
    from_siblings(diag, mb, m_r, 0)

    def product(buf, half):
        total = None
        for k in range(hc):
            term = dot(buf[k], kcol[pl.ds(half * hs + k * per, per)].reshape(width, width))
            total = term if total is None else total + term
        return total

    @pl.when(diag)
    def _():
        rm[mine] = 1.5 * mb[mine] - 0.5 * product(mb, hseg)

    push(diag, rm.at[mine], rm.at[mine], pair_r.at[1], seg, partner)
    siblings(diag, rm, row_r, 1)

    from_siblings(None, rp, row_r, 0)
    eb[mine] = product(rp, hseg)
    siblings(None, eb, e_r, 0)

    arrive(off, rm.at[mine], pair_r.at[1])
    siblings(off, rm, row_r, 1)
    from_siblings(None, rm, row_r, 1)
    jb[mine] = product(rm, hseg)
    siblings(None, jb, e_r, 1)

    settle(2, True)
    settle(2, False)
    settle(3, True)
    settle(3, False)
    from_siblings(None, eb, e_r, 0)
    coupling = 1.5 * eb[mine] - 0.5 * product(eb, hcol)
    defect = identity - coupling
    sq1[seg, pl.ds(8, 8)] = fold(defect * defect)
    for d in range(1, nseg):
        push(None, sq1.at[seg], sq1.at[seg], q1_r.at[seg], lax.rem(seg + d, nseg), col)

    from_siblings(None, jb, e_r, 1)
    tail = 1.5 * jb[mine] - 0.5 * product(jb, hcol)

    @pl.when(diag)
    def _():
        out_ref[...] = 1.5 * mb[mine] - 0.5 * tail

    @pl.when(off)
    def _():
        out_ref[...] = -0.5 * tail

    for d in range(1, nseg):
        k = lax.rem(seg + d, nseg)
        arrive(None, sq1.at[k], q1_r.at[k])
    sq2[col] = jnp.sum(sq1[...], axis=0)
    for d in range(1, ncol):
        push(None, sq2.at[col], sq2.at[col], q2_r.at[col], seg, lax.rem(col + d, ncol))
    for d in range(1, ncol):
        k = lax.rem(col + d, ncol)
        arrive(None, sq2.at[k], q2_r.at[k])
    tiles = jnp.sum(sq2[...], axis=0)
    for level in range(2):
        amount = jnp.sum(tiles[8 * level:8 * level + 8], axis=(0, 1), keepdims=True)
        err_ref[pl.ds(level, 1)] = jnp.broadcast_to(jnp.sqrt(amount / order), (1, 128))

    for cond, copy in pending:
        if cond is None:
            copy.wait_send()
        else:
            pl.when(cond)(copy.wait_send)


def body(nseg, ncol, margin, leaf_factor):
    rows, width = leaf_factor.shape
    order = margin.shape[1]
    nx, cq, hc = nseg // 4, ncol // 4, ncol // 2
    dma = pltpu.SemaphoreType.DMA
    factor, errors = pl.pallas_call(
        functools.partial(kernel, nseg, ncol, order),
        out_shape=(
            jax.ShapeDtypeStruct((rows, width), F32),
            jax.ShapeDtypeStruct((2, 128), F32),
        ),
        in_specs=[pl.BlockSpec(memory_space=pl.ANY), pl.BlockSpec(memory_space=pltpu.VMEM)],
        out_specs=(pl.BlockSpec(memory_space=pltpu.VMEM),) * 2,
        scratch_shapes=[
            pltpu.VMEM((rows, nx * rows), F32),
            pltpu.VMEM((nx, rows, width), F32),
            pltpu.VMEM((cq, rows, width), F32),
            pltpu.VMEM((nx, rows, width), F32),
            pltpu.VMEM((nx, rows, width), F32),
            pltpu.VMEM((nseg, rows, width), F32),
            pltpu.VMEM((hc, rows, width), F32),
            pltpu.VMEM((hc, rows, width), F32),
            pltpu.VMEM((hc, rows, width), F32),
            pltpu.VMEM((hc, rows, width), F32),
            pltpu.VMEM((hc, rows, width), F32),
            pltpu.VMEM((nseg, 16, 128), F32),
            pltpu.VMEM((ncol, 16, 128), F32),
            dma((SENDS + 16 * nseg,)),
            dma((CHUNKS,)),
            dma((nx, CHUNKS)),
            dma((cq,)),
            dma((nx,)),
            dma((4, CHUNKS)),
            dma((nseg, CHUNKS)),
            dma((2, hc)),
            dma((2,)),
            dma((1, hc)),
            dma((2, hc)),
            dma((nseg,)),
            dma((ncol,)),
            dma((1,)),
        ],
        compiler_params=pltpu.CompilerParams(
            collective_id=0, has_side_effects=True, vmem_limit_bytes=56 * 1024 * 1024
        ),
    )(margin, leaf_factor)
    return factor, errors[:, 0]


def solution(mesh):
    return jax.shard_map(
        functools.partial(body, mesh.shape["seg"], mesh.shape["col"]),
        mesh=mesh,
        in_specs=(P("seg", None), P("seg", "col")),
        out_specs=(P("seg", "col"), P()),
        check_vma=False,
    )
```

```python
import functools

import jax
import jax.numpy as jnp
from jax import lax
from jax.experimental import pallas as pl
from jax.experimental.pallas import tpu as pltpu
from jax.sharding import PartitionSpec as P

MESH = pl.DeviceIdType.MESH
F32 = jnp.float32
CHUNKS = 3
SENDS = 128


def dot(left, right, left_dim=1):
    return lax.dot_general(
        left,
        right,
        (((left_dim,), (0,)), ((), ())),
        precision=lax.Precision.HIGHEST,
        preferred_element_type=F32,
    )


def parts(values):
    high = values.astype(jnp.bfloat16)
    return high, (values - high.astype(F32)).astype(jnp.bfloat16)


def dot3(left, right):
    rows = left.shape[0]
    left_high, left_low = parts(left)
    right_high, right_low = parts(right)
    both = jnp.dot(jnp.concatenate([left_high, left_low], axis=0), right_high, preferred_element_type=F32)
    rest = jnp.dot(left_high, right_low, preferred_element_type=F32)
    return both[:rows] + (both[rows:] + rest)


def fold(values):
    rows, width = values.shape
    tall = jnp.sum(values.reshape(rows // 8, 8, width), axis=0)
    total = tall[:, :128]
    for start in range(128, width, 128):
        total = total + tall[:, start:start + 128]
    return total


def kernel(
    nseg, ncol, order,
    margin_ref, leaf_ref, out_ref, err_ref,
    sblk, lcol, lrow, part, rk, ub, kcol, rp, rm, mb, eb, jb, sq1, sq2,
    send, lz_r, lx_r, lrow_r, rk_r, ub_r, kz_r, kx_r, row_r, pair_r, m_r, e_r, q1_r, q2_r, local,
):
    rows, width = leaf_ref.shape
    nx = nseg // 4
    cq = ncol // 4
    hs, hc = nseg // 2, ncol // 2
    per = width // rows
    quarter = nx * rows
    step = rows // CHUNKS

    seg = lax.axis_index("seg")
    col = lax.axis_index("col")
    z, x = lax.div(seg, nx), lax.rem(seg, nx)
    qc = lax.div(col, cq)
    hseg, hcol = lax.div(z, 2), lax.div(qc, 2)
    diag = hseg == hcol
    mine = lax.rem(col, hc)
    half_col = col - mine

    pending = []
    used = [0]

    def true():
        return seg >= 0

    def push(cond, src, dst, rsem, to_seg, to_col):
        index = used[0]
        used[0] += 1
        copy = pltpu.make_async_remote_copy(
            src_ref=src, dst_ref=dst, send_sem=send.at[index], recv_sem=rsem,
            device_id=(to_seg, to_col), device_id_type=MESH,
        )
        if cond is None:
            copy.start()
        else:
            pl.when(cond)(copy.start)
        pending.append((cond, copy))

    def arrive(cond, dst, rsem):
        copy = pltpu.make_async_remote_copy(
            src_ref=dst, dst_ref=dst, send_sem=send.at[0], recv_sem=rsem,
            device_id=(seg, lax.rem(col + 1, ncol)), device_id_type=MESH,
        )
        if cond is None:
            copy.wait_recv()
        else:
            pl.when(cond)(copy.wait_recv)

    def other_x(d):
        return z * nx + lax.rem(x + d, nx)

    fetch = pltpu.make_async_copy(
        margin_ref.at[:, pl.ds(pl.multiple_of(col * width, 128), width)], sblk, local.at[0]
    )
    fetch.start()
    owner = qc == z
    own_slot = lax.rem(col, cq)

    @pl.when(owner)
    def _():
        lcol[x] = leaf_ref[...]
        lrow[own_slot] = leaf_ref[...]

    barrier = pltpu.get_barrier_semaphore()
    for d in range(1, nseg):
        pl.semaphore_signal(barrier, inc=1, device_id=(lax.rem(seg + d, nseg), col), device_id_type=MESH)
    for d in range(1, ncol):
        pl.semaphore_signal(barrier, inc=1, device_id=(seg, lax.rem(col + d, ncol)), device_id_type=MESH)
    pl.semaphore_wait(barrier, nseg + ncol - 2)

    mate = col + 1 - 2 * lax.rem(col, 2)
    for j in range(CHUNKS):
        here = pl.ds(j * step, step)
        for k in range(cq):
            home = z * cq + k
            lead = lax.rem(col, 2) == lax.rem(home, 2)
            block = lrow.at[k, here]
            for d in range(2, ncol, 2):
                push(col == home, block, block, lrow_r.at[k, j], seg, lax.rem(col + d, ncol))
            arrive(lead & (col != home), block, lrow_r.at[k, j])
            push(lead, block, block, lrow_r.at[k, j], seg, mate)
    for j in range(CHUNKS):
        block = lcol.at[x, pl.ds(j * step, step)]
        push(owner & (z < 3), block, block, lz_r.at[j], seg + nx, col)
        push(owner & (z > 0), block, block, lz_r.at[j], seg - nx, col)
    fetch.wait()
    for j in range(CHUNKS):
        for k in range(cq):
            lead = lax.rem(col, 2) == lax.rem(z * cq + k, 2)
            arrive(jnp.logical_not(lead), lrow.at[k, pl.ds(j * step, step)], lrow_r.at[k, j])
    for k in range(cq):
        piece = dot(lrow[k], sblk[...], 0)
        part[pl.ds(k * per, per)] = piece.reshape(per, rows, width)
    for j in range(CHUNKS):
        here = pl.ds(j * step, step)
        for d in range(1, nx):
            to_x = jnp.minimum(x + d, nx - 1)
            push(x + d < nx, part.at[to_x, here], rk.at[x, here], rk_r.at[x, j], z * nx + to_x, col)
    for j in range(CHUNKS):
        block = lcol.at[x, pl.ds(j * step, step)]
        arrive(jnp.logical_not(owner), block, lz_r.at[j])
        push((z > qc) & (z < 3), block, block, lz_r.at[j], seg + nx, col)
        push((z < qc) & (z > 0), block, block, lz_r.at[j], seg - nx, col)
        for d in range(1, nx):
            push(None, block, block, lx_r.at[x, j], other_x(d), col)
    for d in range(1, nx):
        from_x = lax.rem(x + d, nx)
        for j in range(CHUNKS):
            arrive(None, lcol.at[from_x, pl.ds(j * step, step)], lx_r.at[from_x, j])

    def form(j):
        here = pl.ds(j * step, step)
        ub[own_slot, here] = part[x, here]
        for d in range(1, nx):
            from_x = jnp.maximum(x - d, 0)
            arrive(x >= d, rk.at[from_x, here], rk_r.at[from_x, j])

            @pl.when(x >= d)
            def _():
                ub[own_slot, here] += rk[from_x, here]

        first = col - own_slot
        for d in range(1, cq):
            block = ub.at[own_slot, here]
            push(None, block, block, ub_r.at[own_slot, j], seg, first + lax.rem(own_slot + d, cq))
        for d in range(1, cq):
            k = lax.rem(own_slot + d, cq)
            arrive(None, ub.at[k, here], ub_r.at[k, j])
        total = None
        for k in range(cq):
            term = dot(ub[k, here], lcol[pl.ds(k * per, per)].reshape(width, width))
            total = term if total is None else total + term
        kcol[seg, here] = total

    def spread(distance, up):
        origin = z - distance if up else z + distance
        valid = (origin >= 0) & (origin <= 3)
        wide = lax.div(origin, 2) == hcol
        same = lax.div(origin, 2) == hseg
        reached = valid & (wide | same)
        low = jnp.where(wide, 0, 2 * hseg)
        high = jnp.where(wide, 3, 2 * hseg + 1)
        slot = jnp.clip(origin, 0, 3) * nx + x
        plane = jnp.clip(origin, 0, 3)
        for j in range(CHUNKS):
            block = kcol.at[slot, pl.ds(j * step, step)]
            if distance == 0:
                form(j)
            if distance:
                arrive(reached, block, kz_r.at[plane, j])
            if up or distance == 0:
                push(reached & (z < high), block, block, kz_r.at[plane, j], seg + nx, col)
            if not up or distance == 0:
                push(reached & (z > low), block, block, kz_r.at[plane, j], seg - nx, col)
            for d in range(1, nx):
                push(reached, block, block, kx_r.at[slot, j], other_x(d), col)

    def settle(distance, up):
        origin = z - distance if up else z + distance
        valid = (origin >= 0) & (origin <= 3)
        reached = valid & ((lax.div(origin, 2) == hcol) | (lax.div(origin, 2) == hseg))
        for d in range(1, nx):
            slot = jnp.clip(origin, 0, 3) * nx + lax.rem(x + d, nx)
            for j in range(CHUNKS):
                arrive(reached, kcol.at[slot, pl.ds(j * step, step)], kx_r.at[slot, j])

    spread(0, False)

    partner = lax.rem(col + hc, ncol)
    row_ids = seg * rows + lax.broadcasted_iota(jnp.int32, (rows, width), 0)
    col_ids = col * width + lax.broadcasted_iota(jnp.int32, (rows, width), 1)
    identity = (row_ids == col_ids).astype(F32)

    def siblings(cond, buf, rsem, which):
        for d in range(1, hc):
            push(cond, buf.at[mine], buf.at[mine], rsem.at[which, mine], seg, half_col + lax.rem(mine + d, hc))

    def from_siblings(cond, buf, rsem, which):
        for d in range(1, hc):
            k = lax.rem(mine + d, hc)
            arrive(cond, buf.at[k], rsem.at[which, k])

    @pl.when(diag)
    def _():
        own = kcol[seg]
        defect = identity - own
        sq1[seg, pl.ds(0, 8)] = fold(defect * defect)
        rp[mine] = 1.5 * identity - 0.5 * own

    @pl.when(jnp.logical_not(diag))
    def _():
        sq1[seg, pl.ds(0, 8)] = jnp.zeros((8, 128), F32)

    push(diag, rp.at[mine], rp.at[mine], pair_r.at[0], seg, partner)
    siblings(diag, rp, row_r, 0)

    spread(1, True)
    spread(1, False)
    spread(2, True)
    spread(2, False)
    spread(3, True)
    spread(3, False)
    off = jnp.logical_not(diag)
    arrive(off, rp.at[mine], pair_r.at[0])
    siblings(off, rp, row_r, 0)

    settle(0, False)

    @pl.when(diag)
    def _():
        near = kcol[pl.ds(z * nx, nx)].reshape(quarter, width)
        update = jnp.zeros((rows, width), F32)
        for k in range(cq):
            update = update + dot3(lrow[k], near[k * width:(k + 1) * width])
        mb[mine] = 1.5 * leaf_ref[...] - 0.5 * update

    siblings(diag, mb, m_r, 0)
    settle(1, True)
    settle(1, False)
    from_siblings(diag, mb, m_r, 0)

    def product(buf, half):
        total = None
        for k in range(hc):
            term = dot3(buf[k], kcol[pl.ds(half * hs + k * per, per)].reshape(width, width))
            total = term if total is None else total + term
        return total

    @pl.when(diag)
    def _():
        rm[mine] = 1.5 * mb[mine] - 0.5 * product(mb, hseg)

    push(diag, rm.at[mine], rm.at[mine], pair_r.at[1], seg, partner)
    siblings(diag, rm, row_r, 1)

    from_siblings(None, rp, row_r, 0)
    eb[mine] = product(rp, hseg)
    siblings(None, eb, e_r, 0)

    arrive(off, rm.at[mine], pair_r.at[1])
    siblings(off, rm, row_r, 1)
    from_siblings(None, rm, row_r, 1)
    jb[mine] = product(rm, hseg)
    siblings(None, jb, e_r, 1)

    settle(2, True)
    settle(2, False)
    settle(3, True)
    settle(3, False)
    from_siblings(None, eb, e_r, 0)
    coupling = 1.5 * eb[mine] - 0.5 * product(eb, hcol)
    defect = identity - coupling
    sq1[seg, pl.ds(8, 8)] = fold(defect * defect)
    for d in range(1, nseg):
        push(None, sq1.at[seg], sq1.at[seg], q1_r.at[seg], lax.rem(seg + d, nseg), col)

    from_siblings(None, jb, e_r, 1)
    tail = 1.5 * jb[mine] - 0.5 * product(jb, hcol)

    @pl.when(diag)
    def _():
        out_ref[...] = 1.5 * mb[mine] - 0.5 * tail

    @pl.when(off)
    def _():
        out_ref[...] = -0.5 * tail

    for d in range(1, nseg):
        k = lax.rem(seg + d, nseg)
        arrive(None, sq1.at[k], q1_r.at[k])
    sq2[col] = jnp.sum(sq1[...], axis=0)
    for d in range(1, ncol):
        push(None, sq2.at[col], sq2.at[col], q2_r.at[col], seg, lax.rem(col + d, ncol))
    for d in range(1, ncol):
        k = lax.rem(col + d, ncol)
        arrive(None, sq2.at[k], q2_r.at[k])
    tiles = jnp.sum(sq2[...], axis=0)
    for level in range(2):
        amount = jnp.sum(tiles[8 * level:8 * level + 8], axis=(0, 1), keepdims=True)
        err_ref[level] = jnp.sqrt(amount / order)[0, 0]

    for cond, copy in pending:
        if cond is None:
            copy.wait_send()
        else:
            pl.when(cond)(copy.wait_send)


def body(nseg, ncol, margin, leaf_factor):
    rows, width = leaf_factor.shape
    order = margin.shape[1]
    nx, cq, hc = nseg // 4, ncol // 4, ncol // 2
    dma = pltpu.SemaphoreType.DMA
    factor, errors = pl.pallas_call(
        functools.partial(kernel, nseg, ncol, order),
        out_shape=(
            jax.ShapeDtypeStruct((rows, width), F32),
            jax.ShapeDtypeStruct((2,), F32),
        ),
        in_specs=[pl.BlockSpec(memory_space=pl.ANY), pl.BlockSpec(memory_space=pltpu.VMEM)],
        out_specs=(pl.BlockSpec(memory_space=pltpu.VMEM), pl.BlockSpec(memory_space=pltpu.SMEM)),
        scratch_shapes=[
            pltpu.VMEM((rows, width), F32),
            pltpu.VMEM((nx, rows, width), F32),
            pltpu.VMEM((cq, rows, width), F32),
            pltpu.VMEM((nx, rows, width), F32),
            pltpu.VMEM((nx, rows, width), F32),
            pltpu.VMEM((cq, rows, width), F32),
            pltpu.VMEM((nseg, rows, width), F32),
            pltpu.VMEM((hc, rows, width), F32),
            pltpu.VMEM((hc, rows, width), F32),
            pltpu.VMEM((hc, rows, width), F32),
            pltpu.VMEM((hc, rows, width), F32),
            pltpu.VMEM((hc, rows, width), F32),
            pltpu.VMEM((nseg, 16, 128), F32),
            pltpu.VMEM((ncol, 16, 128), F32),
            dma((SENDS + 16 * nseg,)),
            dma((CHUNKS,)),
            dma((nx, CHUNKS)),
            dma((cq, CHUNKS)),
            dma((nx, CHUNKS)),
            dma((cq, CHUNKS)),
            dma((4, CHUNKS)),
            dma((nseg, CHUNKS)),
            dma((2, hc)),
            dma((2,)),
            dma((1, hc)),
            dma((2, hc)),
            dma((nseg,)),
            dma((ncol,)),
            dma((1,)),
        ],
        compiler_params=pltpu.CompilerParams(
            collective_id=0, has_side_effects=True, vmem_limit_bytes=56 * 1024 * 1024
        ),
    )(margin, leaf_factor)
    return factor, errors


def solution(mesh):
    return jax.shard_map(
        functools.partial(body, mesh.shape["seg"], mesh.shape["col"]),
        mesh=mesh,
        in_specs=(P("seg", None), P("seg", "col")),
        out_specs=(P("seg", "col"), P()),
        check_vma=False,
    )
```

```python
import functools

import jax
import jax.numpy as jnp
from jax import lax
from jax.experimental import pallas as pl
from jax.experimental.pallas import tpu as pltpu
from jax.sharding import PartitionSpec as P

MESH = pl.DeviceIdType.MESH
F32 = jnp.float32
CHUNKS = 3
SENDS = 128


def dot(left, right, left_dim=1):
    return lax.dot_general(
        left,
        right,
        (((left_dim,), (0,)), ((), ())),
        precision=lax.Precision.HIGHEST,
        preferred_element_type=F32,
    )


def parts(values):
    high = values.astype(jnp.bfloat16)
    return high, (values - high.astype(F32)).astype(jnp.bfloat16)


def dot3(left, right):
    rows = left.shape[0]
    left_high, left_low = parts(left)
    right_high, right_low = parts(right)
    both = jnp.dot(jnp.concatenate([left_high, left_low], axis=0), right_high, preferred_element_type=F32)
    rest = jnp.dot(left_high, right_low, preferred_element_type=F32)
    return both[:rows] + (both[rows:] + rest)


def fold(values):
    rows, width = values.shape
    tall = jnp.sum(values.reshape(rows // 8, 8, width), axis=0)
    total = tall[:, :128]
    for start in range(128, width, 128):
        total = total + tall[:, start:start + 128]
    return total


def kernel(
    nseg, ncol, order,
    margin_ref, leaf_ref, out_ref, err_ref,
    sblk, lcol, lrow, part, rk, ub, kcol, rp, rm, mb, eb, jb, sq1, sq2,
    send, lz_r, lx_r, lrow_r, rk_r, ub_r, kz_r, kx_r, row_r, pair_r, m_r, e_r, q1_r, q2_r, local,
):
    rows, width = leaf_ref.shape
    nx = nseg // 4
    cq = ncol // 4
    hs, hc = nseg // 2, ncol // 2
    per = width // rows
    quarter = nx * rows
    step = rows // CHUNKS

    seg = lax.axis_index("seg")
    col = lax.axis_index("col")
    z, x = lax.div(seg, nx), lax.rem(seg, nx)
    qc = lax.div(col, cq)
    hseg, hcol = lax.div(z, 2), lax.div(qc, 2)
    diag = hseg == hcol
    mine = lax.rem(col, hc)
    half_col = col - mine

    pending = []
    used = [0]

    def true():
        return seg >= 0

    def push(cond, src, dst, rsem, to_seg, to_col):
        index = used[0]
        used[0] += 1
        copy = pltpu.make_async_remote_copy(
            src_ref=src, dst_ref=dst, send_sem=send.at[index], recv_sem=rsem,
            device_id=(to_seg, to_col), device_id_type=MESH,
        )
        if cond is None:
            copy.start()
        else:
            pl.when(cond)(copy.start)
        pending.append((cond, copy))

    def arrive(cond, dst, rsem):
        copy = pltpu.make_async_remote_copy(
            src_ref=dst, dst_ref=dst, send_sem=send.at[0], recv_sem=rsem,
            device_id=(seg, lax.rem(col + 1, ncol)), device_id_type=MESH,
        )
        if cond is None:
            copy.wait_recv()
        else:
            pl.when(cond)(copy.wait_recv)

    def other_x(d):
        return z * nx + lax.rem(x + d, nx)

    fetch = pltpu.make_async_copy(
        margin_ref.at[:, pl.ds(pl.multiple_of(col * width, 128), width)], sblk, local.at[0]
    )
    fetch.start()
    owner = qc == z
    own_slot = lax.rem(col, cq)

    @pl.when(owner)
    def _():
        lcol[x] = leaf_ref[...]
        lrow[own_slot] = leaf_ref[...]

    barrier = pltpu.get_barrier_semaphore()
    for d in range(1, nseg):
        pl.semaphore_signal(barrier, inc=1, device_id=(lax.rem(seg + d, nseg), col), device_id_type=MESH)
    for d in range(1, ncol):
        pl.semaphore_signal(barrier, inc=1, device_id=(seg, lax.rem(col + d, ncol)), device_id_type=MESH)
    pl.semaphore_wait(barrier, nseg + ncol - 2)

    mate = col + 1 - 2 * lax.rem(col, 2)
    for j in range(CHUNKS):
        here = pl.ds(j * step, step)
        for k in range(cq):
            home = z * cq + k
            lead = lax.rem(col, 2) == lax.rem(home, 2)
            block = lrow.at[k, here]
            for d in range(2, ncol, 2):
                push(col == home, block, block, lrow_r.at[k, j], seg, lax.rem(col + d, ncol))
            arrive(lead & (col != home), block, lrow_r.at[k, j])
            push(lead, block, block, lrow_r.at[k, j], seg, mate)
    near = (z - qc <= 1) & (qc - z <= 1)

    def pass_on(chosen):
        for j in range(CHUNKS):
            block = lcol.at[x, pl.ds(j * step, step)]
            arrive(chosen & jnp.logical_not(owner), block, lz_r.at[j])
            push(chosen & (z >= qc) & (z < 3), block, block, lz_r.at[j], seg + nx, col)
            push(chosen & (z <= qc) & (z > 0), block, block, lz_r.at[j], seg - nx, col)
            for d in range(1, nx):
                push(chosen, block, block, lx_r.at[x, j], other_x(d), col)

    pass_on(near)
    fetch.wait()
    for j in range(CHUNKS):
        for k in range(cq):
            lead = lax.rem(col, 2) == lax.rem(z * cq + k, 2)
            arrive(jnp.logical_not(lead), lrow.at[k, pl.ds(j * step, step)], lrow_r.at[k, j])
    for k in range(cq):
        piece = dot(lrow[k], sblk[...], 0)
        part[pl.ds(k * per, per)] = piece.reshape(per, rows, width)
    for j in range(CHUNKS):
        here = pl.ds(j * step, step)
        for d in range(1, nx):
            to_x = jnp.minimum(x + d, nx - 1)
            push(x + d < nx, part.at[to_x, here], rk.at[x, here], rk_r.at[x, j], z * nx + to_x, col)
    pass_on(jnp.logical_not(near))
    for d in range(1, nx):
        from_x = lax.rem(x + d, nx)
        for j in range(CHUNKS):
            arrive(None, lcol.at[from_x, pl.ds(j * step, step)], lx_r.at[from_x, j])

    def form(j):
        here = pl.ds(j * step, step)
        ub[own_slot, here] = part[x, here]
        for d in range(1, nx):
            from_x = jnp.maximum(x - d, 0)
            arrive(x >= d, rk.at[from_x, here], rk_r.at[from_x, j])

            @pl.when(x >= d)
            def _():
                ub[own_slot, here] += rk[from_x, here]

        first = col - own_slot
        for d in range(1, cq):
            block = ub.at[own_slot, here]
            push(None, block, block, ub_r.at[own_slot, j], seg, first + lax.rem(own_slot + d, cq))
        for d in range(1, cq):
            k = lax.rem(own_slot + d, cq)
            arrive(None, ub.at[k, here], ub_r.at[k, j])
        total = None
        for k in range(cq):
            term = dot(ub[k, here], lcol[pl.ds(k * per, per)].reshape(width, width))
            total = term if total is None else total + term
        kcol[seg, here] = total

    def spread(distance, up, j):
        origin = z - distance if up else z + distance
        valid = (origin >= 0) & (origin <= 3)
        wide = lax.div(origin, 2) == hcol
        same = lax.div(origin, 2) == hseg
        reached = valid & (wide | same)
        low = jnp.where(wide, 0, 2 * hseg)
        high = jnp.where(wide, 3, 2 * hseg + 1)
        plane = jnp.clip(origin, 0, 3)
        slot = plane * nx + x
        block = kcol.at[slot, pl.ds(j * step, step)]
        if distance:
            arrive(reached, block, kz_r.at[plane, j])
        if up or distance == 0:
            push(reached & (z < high), block, block, kz_r.at[plane, j], seg + nx, col)
        if not up or distance == 0:
            push(reached & (z > low), block, block, kz_r.at[plane, j], seg - nx, col)
        if distance < 2:
            across = None if distance == 0 else reached & jnp.logical_not(same)
        else:
            across = reached
        for d in range(1, nx):
            push(across, block, block, kx_r.at[slot, j], other_x(d), col)

    def settle(distance, up, j, inside):
        origin = z - distance if up else z + distance
        valid = (origin >= 0) & (origin <= 3)
        same = lax.div(origin, 2) == hseg
        wide = lax.div(origin, 2) == hcol
        reached = valid & (same if inside else wide & jnp.logical_not(same))
        for d in range(1, nx):
            slot = jnp.clip(origin, 0, 3) * nx + lax.rem(x + d, nx)
            arrive(reached, kcol.at[slot, pl.ds(j * step, step)], kx_r.at[slot, j])

    def relay(j):
        sibling = 2 * hseg + 1 - lax.rem(z, 2)
        for d in range(1, nx):
            slot = z * nx + lax.rem(x + d, nx)
            block = kcol.at[slot, pl.ds(j * step, step)]
            arrive(None, block, kx_r.at[slot, j])
            push(None, block, block, kx_r.at[slot, j], sibling * nx + x, col)

    for j in range(CHUNKS):
        form(j)
        spread(0, False, j)

    partner = lax.rem(col + hc, ncol)
    row_ids = seg * rows + lax.broadcasted_iota(jnp.int32, (rows, width), 0)
    col_ids = col * width + lax.broadcasted_iota(jnp.int32, (rows, width), 1)
    identity = (row_ids == col_ids).astype(F32)

    def siblings(cond, buf, rsem, which):
        for d in range(1, hc):
            push(cond, buf.at[mine], buf.at[mine], rsem.at[which, mine], seg, half_col + lax.rem(mine + d, hc))

    def from_siblings(cond, buf, rsem, which):
        for d in range(1, hc):
            k = lax.rem(mine + d, hc)
            arrive(cond, buf.at[k], rsem.at[which, k])

    @pl.when(diag)
    def _():
        own = kcol[seg]
        defect = identity - own
        sq1[seg, pl.ds(0, 8)] = fold(defect * defect)
        rp[mine] = 1.5 * identity - 0.5 * own

    @pl.when(jnp.logical_not(diag))
    def _():
        sq1[seg, pl.ds(0, 8)] = jnp.zeros((8, 128), F32)

    push(diag, rp.at[mine], rp.at[mine], pair_r.at[0], seg, partner)
    siblings(diag, rp, row_r, 0)

    off = jnp.logical_not(diag)
    for j in range(CHUNKS):
        spread(1, True, j)
        spread(1, False, j)
    for j in range(CHUNKS):
        relay(j)
        spread(2, True, j)
        spread(2, False, j)
    arrive(off, rp.at[mine], pair_r.at[0])
    siblings(off, rp, row_r, 0)

    @pl.when(diag)
    def _():
        plane = kcol[pl.ds(z * nx, nx)].reshape(quarter, width)
        update = jnp.zeros((rows, width), F32)
        for k in range(cq):
            update = update + dot3(lrow[k], plane[k * width:(k + 1) * width])
        mb[mine] = 1.5 * leaf_ref[...] - 0.5 * update

    siblings(diag, mb, m_r, 0)
    for j in range(CHUNKS):
        settle(1, True, j, True)
        settle(1, False, j, True)
    from_siblings(diag, mb, m_r, 0)

    def product(buf, half):
        total = None
        for k in range(hc):
            term = dot3(buf[k], kcol[pl.ds(half * hs + k * per, per)].reshape(width, width))
            total = term if total is None else total + term
        return total

    @pl.when(diag)
    def _():
        rm[mine] = 1.5 * mb[mine] - 0.5 * product(mb, hseg)

    push(diag, rm.at[mine], rm.at[mine], pair_r.at[1], seg, partner)
    siblings(diag, rm, row_r, 1)

    from_siblings(None, rp, row_r, 0)
    eb[mine] = product(rp, hseg)
    siblings(None, eb, e_r, 0)
    for j in range(CHUNKS):
        spread(3, True, j)
        spread(3, False, j)

    arrive(off, rm.at[mine], pair_r.at[1])
    siblings(off, rm, row_r, 1)
    from_siblings(None, rm, row_r, 1)
    jb[mine] = product(rm, hseg)
    siblings(None, jb, e_r, 1)

    for distance in (1, 2, 3):
        for j in range(CHUNKS):
            settle(distance, True, j, False)
            settle(distance, False, j, False)
    from_siblings(None, eb, e_r, 0)
    coupling = 1.5 * eb[mine] - 0.5 * product(eb, hcol)
    defect = identity - coupling
    sq1[seg, pl.ds(8, 8)] = fold(defect * defect)
    for d in range(1, nseg):
        push(None, sq1.at[seg], sq1.at[seg], q1_r.at[seg], lax.rem(seg + d, nseg), col)

    from_siblings(None, jb, e_r, 1)
    tail = 1.5 * jb[mine] - 0.5 * product(jb, hcol)

    @pl.when(diag)
    def _():
        out_ref[...] = 1.5 * mb[mine] - 0.5 * tail

    @pl.when(off)
    def _():
        out_ref[...] = -0.5 * tail

    for d in range(1, nseg):
        k = lax.rem(seg + d, nseg)
        arrive(None, sq1.at[k], q1_r.at[k])
    sq2[col] = jnp.sum(sq1[...], axis=0)
    for d in range(1, ncol):
        push(None, sq2.at[col], sq2.at[col], q2_r.at[col], seg, lax.rem(col + d, ncol))
    for d in range(1, ncol):
        k = lax.rem(col + d, ncol)
        arrive(None, sq2.at[k], q2_r.at[k])
    tiles = jnp.sum(sq2[...], axis=0)
    for level in range(2):
        amount = jnp.sum(tiles[8 * level:8 * level + 8], axis=(0, 1), keepdims=True)
        err_ref[level] = jnp.sqrt(amount / order)[0, 0]

    for cond, copy in pending:
        if cond is None:
            copy.wait_send()
        else:
            pl.when(cond)(copy.wait_send)


def body(nseg, ncol, margin, leaf_factor):
    rows, width = leaf_factor.shape
    order = margin.shape[1]
    nx, cq, hc = nseg // 4, ncol // 4, ncol // 2
    dma = pltpu.SemaphoreType.DMA
    factor, errors = pl.pallas_call(
        functools.partial(kernel, nseg, ncol, order),
        out_shape=(
            jax.ShapeDtypeStruct((rows, width), F32),
            jax.ShapeDtypeStruct((2,), F32),
        ),
        in_specs=[pl.BlockSpec(memory_space=pl.ANY), pl.BlockSpec(memory_space=pltpu.VMEM)],
        out_specs=(pl.BlockSpec(memory_space=pltpu.VMEM), pl.BlockSpec(memory_space=pltpu.SMEM)),
        scratch_shapes=[
            pltpu.VMEM((rows, width), F32),
            pltpu.VMEM((nx, rows, width), F32),
            pltpu.VMEM((cq, rows, width), F32),
            pltpu.VMEM((nx, rows, width), F32),
            pltpu.VMEM((nx, rows, width), F32),
            pltpu.VMEM((cq, rows, width), F32),
            pltpu.VMEM((nseg, rows, width), F32),
            pltpu.VMEM((hc, rows, width), F32),
            pltpu.VMEM((hc, rows, width), F32),
            pltpu.VMEM((hc, rows, width), F32),
            pltpu.VMEM((hc, rows, width), F32),
            pltpu.VMEM((hc, rows, width), F32),
            pltpu.VMEM((nseg, 16, 128), F32),
            pltpu.VMEM((ncol, 16, 128), F32),
            dma((SENDS + 16 * nseg,)),
            dma((CHUNKS,)),
            dma((nx, CHUNKS)),
            dma((cq, CHUNKS)),
            dma((nx, CHUNKS)),
            dma((cq, CHUNKS)),
            dma((4, CHUNKS)),
            dma((nseg, CHUNKS)),
            dma((2, hc)),
            dma((2,)),
            dma((1, hc)),
            dma((2, hc)),
            dma((nseg,)),
            dma((ncol,)),
            dma((1,)),
        ],
        compiler_params=pltpu.CompilerParams(
            collective_id=0, has_side_effects=True, vmem_limit_bytes=56 * 1024 * 1024
        ),
    )(margin, leaf_factor)
    return factor, errors


def solution(mesh):
    return jax.shard_map(
        functools.partial(body, mesh.shape["seg"], mesh.shape["col"]),
        mesh=mesh,
        in_specs=(P("seg", None), P("seg", "col")),
        out_specs=(P("seg", "col"), P()),
        check_vma=False,
    )
```

```python
import functools

import jax
import jax.numpy as jnp
from jax import lax
from jax.experimental import pallas as pl
from jax.experimental.pallas import tpu as pltpu
from jax.sharding import PartitionSpec as P

MESH = pl.DeviceIdType.MESH
F32 = jnp.float32
CHUNKS = 3
RELAYED = 1
SENDS = 128


def dot(left, right, left_dim=1):
    return lax.dot_general(
        left,
        right,
        (((left_dim,), (0,)), ((), ())),
        precision=lax.Precision.HIGHEST,
        preferred_element_type=F32,
    )


def parts(values):
    high = values.astype(jnp.bfloat16)
    return high, (values - high.astype(F32)).astype(jnp.bfloat16)


def dot3(left, right):
    rows = left.shape[0]
    left_high, left_low = parts(left)
    right_high, right_low = parts(right)
    both = jnp.dot(jnp.concatenate([left_high, left_low], axis=0), right_high, preferred_element_type=F32)
    rest = jnp.dot(left_high, right_low, preferred_element_type=F32)
    return both[:rows] + (both[rows:] + rest)


def fold(values):
    rows, width = values.shape
    tall = jnp.sum(values.reshape(rows // 8, 8, width), axis=0)
    total = tall[:, :128]
    for start in range(128, width, 128):
        total = total + tall[:, start:start + 128]
    return total


def kernel(
    nseg, ncol, order,
    margin_ref, leaf_ref, out_ref, err_ref,
    sblk, lcol, lrow, part, rk, ub, kcol, rp, rm, mb, eb, jb, sq1, sq2,
    send, lz_r, lrow_r, rk_r, ub_r, kz_r, kx_r, row_r, pair_r, m_r, e_r, q1_r, q2_r, local,
):
    rows, width = leaf_ref.shape
    nx = nseg // 4
    cq = ncol // 4
    hs, hc = nseg // 2, ncol // 2
    per = width // rows
    quarter = nx * rows
    step = rows // CHUNKS

    seg = lax.axis_index("seg")
    col = lax.axis_index("col")
    z, x = lax.div(seg, nx), lax.rem(seg, nx)
    qc = lax.div(col, cq)
    hseg, hcol = lax.div(z, 2), lax.div(qc, 2)
    diag = hseg == hcol
    mine = lax.rem(col, hc)
    half_col = col - mine

    pending = []
    used = [0]

    def true():
        return seg >= 0

    def push(cond, src, dst, rsem, to_seg, to_col):
        index = used[0]
        used[0] += 1
        copy = pltpu.make_async_remote_copy(
            src_ref=src, dst_ref=dst, send_sem=send.at[index], recv_sem=rsem,
            device_id=(to_seg, to_col), device_id_type=MESH,
        )
        if cond is None:
            copy.start()
        else:
            pl.when(cond)(copy.start)
        pending.append((cond, copy))

    def arrive(cond, dst, rsem):
        copy = pltpu.make_async_remote_copy(
            src_ref=dst, dst_ref=dst, send_sem=send.at[0], recv_sem=rsem,
            device_id=(seg, lax.rem(col + 1, ncol)), device_id_type=MESH,
        )
        if cond is None:
            copy.wait_recv()
        else:
            pl.when(cond)(copy.wait_recv)

    def other_x(d):
        return z * nx + lax.rem(x + d, nx)

    fetch = pltpu.make_async_copy(
        margin_ref.at[:, pl.ds(pl.multiple_of(col * width, 128), width)], sblk, local.at[0]
    )
    fetch.start()
    owner = qc == z
    own_slot = lax.rem(col, cq)

    @pl.when(owner)
    def _():
        lcol[x] = leaf_ref[...]
        lrow[own_slot] = leaf_ref[...]

    barrier = pltpu.get_barrier_semaphore()
    for d in range(1, nseg):
        pl.semaphore_signal(barrier, inc=1, device_id=(lax.rem(seg + d, nseg), col), device_id_type=MESH)
    for d in range(1, ncol):
        pl.semaphore_signal(barrier, inc=1, device_id=(seg, lax.rem(col + d, ncol)), device_id_type=MESH)
    pl.semaphore_wait(barrier, nseg + ncol - 2)

    mate = col + 1 - 2 * lax.rem(col, 2)
    for j in range(CHUNKS):
        here = pl.ds(j * step, step)
        for k in range(cq):
            home = z * cq + k
            lead = lax.rem(col, 2) == lax.rem(home, 2)
            block = lrow.at[k, here]
            for d in range(2, ncol, 2):
                push(col == home, block, block, lrow_r.at[k, j], seg, lax.rem(col + d, ncol))
            arrive(lead & (col != home), block, lrow_r.at[k, j])
            push(lead, block, block, lrow_r.at[k, j], seg, mate)
    near = (z - qc <= 1) & (qc - z <= 1)

    def pass_on(chosen):
        for d in range(nx):
            slot = jnp.maximum(x - d, 0)
            held = chosen & (x >= d)
            for j in range(CHUNKS):
                block = lcol.at[slot, pl.ds(j * step, step)]
                if d == 0:
                    arrive(held & jnp.logical_not(owner), block, lz_r.at[slot, j])
                else:
                    arrive(held, block, lz_r.at[slot, j])
                push(held & (z >= qc) & (z < 3), block, block, lz_r.at[slot, j], seg + nx, col)
                push(held & (z <= qc) & (z > 0), block, block, lz_r.at[slot, j], seg - nx, col)
                if d == 0:
                    for e in range(1, nx):
                        to_x = lax.rem(x + e, nx)
                        push(chosen & (owner | (to_x < x)), block, block, lz_r.at[slot, j], other_x(e), col)

    pass_on(near)
    fetch.wait()
    for j in range(CHUNKS):
        for k in range(cq):
            lead = lax.rem(col, 2) == lax.rem(z * cq + k, 2)
            arrive(jnp.logical_not(lead), lrow.at[k, pl.ds(j * step, step)], lrow_r.at[k, j])
    for k in range(cq):
        piece = dot(lrow[k], sblk[...], 0)
        part[pl.ds(k * per, per)] = piece.reshape(per, rows, width)
    for j in range(CHUNKS):
        here = pl.ds(j * step, step)
        for d in range(1, nx):
            to_x = jnp.minimum(x + d, nx - 1)
            push(x + d < nx, part.at[to_x, here], rk.at[x, here], rk_r.at[x, j], z * nx + to_x, col)
    pass_on(jnp.logical_not(near))
    for d in range(1, nx):
        from_x = jnp.minimum(x + d, nx - 1)
        for j in range(CHUNKS):
            arrive(x + d < nx, lcol.at[from_x, pl.ds(j * step, step)], lz_r.at[from_x, j])

    def form(j):
        here = pl.ds(j * step, step)
        ub[own_slot, here] = part[x, here]
        for d in range(1, nx):
            from_x = jnp.maximum(x - d, 0)
            arrive(x >= d, rk.at[from_x, here], rk_r.at[from_x, j])

            @pl.when(x >= d)
            def _():
                ub[own_slot, here] += rk[from_x, here]

        first = col - own_slot
        for d in range(1, cq):
            block = ub.at[own_slot, here]
            push(None, block, block, ub_r.at[own_slot, j], seg, first + lax.rem(own_slot + d, cq))
        for d in range(1, cq):
            k = lax.rem(own_slot + d, cq)
            arrive(None, ub.at[k, here], ub_r.at[k, j])
        total = None
        for k in range(cq):
            term = dot(ub[k, here], lcol[pl.ds(k * per, per)].reshape(width, width))
            total = term if total is None else total + term
        kcol[seg, here] = total

    def spread(distance, up, j):
        origin = z - distance if up else z + distance
        valid = (origin >= 0) & (origin <= 3)
        wide = lax.div(origin, 2) == hcol
        same = lax.div(origin, 2) == hseg
        reached = valid & (wide | same)
        low = jnp.where(wide, 0, 2 * hseg)
        high = jnp.where(wide, 3, 2 * hseg + 1)
        plane = jnp.clip(origin, 0, 3)
        slot = plane * nx + x
        block = kcol.at[slot, pl.ds(j * step, step)]
        if distance:
            arrive(reached, block, kz_r.at[plane, j])
        if up or distance == 0:
            push(reached & (z < high), block, block, kz_r.at[plane, j], seg + nx, col)
        if not up or distance == 0:
            push(reached & (z > low), block, block, kz_r.at[plane, j], seg - nx, col)
        across = None if distance == 0 else reached
        if distance == 1 and j < RELAYED:
            across = reached & jnp.logical_not(same)
        for d in range(1, nx):
            push(across, block, block, kx_r.at[slot, j], other_x(d), col)

    def settle(distance, up, j, inside):
        origin = z - distance if up else z + distance
        valid = (origin >= 0) & (origin <= 3)
        same = lax.div(origin, 2) == hseg
        wide = lax.div(origin, 2) == hcol
        reached = valid & (same if inside else wide & jnp.logical_not(same))
        for d in range(1, nx):
            slot = jnp.clip(origin, 0, 3) * nx + lax.rem(x + d, nx)
            arrive(reached, kcol.at[slot, pl.ds(j * step, step)], kx_r.at[slot, j])

    def relay(j):
        sibling = 2 * hseg + 1 - lax.rem(z, 2)
        for d in range(1, nx):
            slot = z * nx + lax.rem(x + d, nx)
            block = kcol.at[slot, pl.ds(j * step, step)]
            arrive(None, block, kx_r.at[slot, j])
            if j < RELAYED:
                push(None, block, block, kx_r.at[slot, j], sibling * nx + x, col)

    for j in range(CHUNKS):
        form(j)
        spread(0, False, j)

    partner = lax.rem(col + hc, ncol)
    row_ids = seg * rows + lax.broadcasted_iota(jnp.int32, (rows, width), 0)
    col_ids = col * width + lax.broadcasted_iota(jnp.int32, (rows, width), 1)
    identity = (row_ids == col_ids).astype(F32)

    def siblings(cond, buf, rsem, which):
        for d in range(1, hc):
            push(cond, buf.at[mine], buf.at[mine], rsem.at[which, mine], seg, half_col + lax.rem(mine + d, hc))

    def from_siblings(cond, buf, rsem, which):
        for d in range(1, hc):
            k = lax.rem(mine + d, hc)
            arrive(cond, buf.at[k], rsem.at[which, k])

    @pl.when(diag)
    def _():
        own = kcol[seg]
        defect = identity - own
        sq1[seg, pl.ds(0, 8)] = fold(defect * defect)
        rp[mine] = 1.5 * identity - 0.5 * own

    @pl.when(jnp.logical_not(diag))
    def _():
        sq1[seg, pl.ds(0, 8)] = jnp.zeros((8, 128), F32)

    push(diag, rp.at[mine], rp.at[mine], pair_r.at[0], seg, partner)
    siblings(diag, rp, row_r, 0)

    off = jnp.logical_not(diag)
    for j in range(CHUNKS):
        spread(1, True, j)
        spread(1, False, j)
    for j in range(CHUNKS):
        relay(j)
        spread(2, True, j)
        spread(2, False, j)
    arrive(off, rp.at[mine], pair_r.at[0])
    siblings(off, rp, row_r, 0)

    @pl.when(diag)
    def _():
        plane = kcol[pl.ds(z * nx, nx)].reshape(quarter, width)
        update = jnp.zeros((rows, width), F32)
        for k in range(cq):
            update = update + dot3(lrow[k], plane[k * width:(k + 1) * width])
        mb[mine] = 1.5 * leaf_ref[...] - 0.5 * update

    siblings(diag, mb, m_r, 0)
    for j in range(CHUNKS):
        settle(1, True, j, True)
        settle(1, False, j, True)
    from_siblings(diag, mb, m_r, 0)

    def product(buf, half):
        total = None
        for k in range(hc):
            term = dot3(buf[k], kcol[pl.ds(half * hs + k * per, per)].reshape(width, width))
            total = term if total is None else total + term
        return total

    @pl.when(diag)
    def _():
        rm[mine] = 1.5 * mb[mine] - 0.5 * product(mb, hseg)

    push(diag, rm.at[mine], rm.at[mine], pair_r.at[1], seg, partner)
    siblings(diag, rm, row_r, 1)

    from_siblings(None, rp, row_r, 0)
    eb[mine] = product(rp, hseg)
    siblings(None, eb, e_r, 0)
    for j in range(CHUNKS):
        spread(3, True, j)
        spread(3, False, j)

    arrive(off, rm.at[mine], pair_r.at[1])
    siblings(off, rm, row_r, 1)
    from_siblings(None, rm, row_r, 1)
    jb[mine] = product(rm, hseg)
    siblings(None, jb, e_r, 1)

    for distance in (1, 2, 3):
        for j in range(CHUNKS):
            settle(distance, True, j, False)
            settle(distance, False, j, False)
    from_siblings(None, eb, e_r, 0)
    coupling = 1.5 * eb[mine] - 0.5 * product(eb, hcol)
    defect = identity - coupling
    sq1[seg, pl.ds(8, 8)] = fold(defect * defect)
    for d in range(1, nseg):
        push(None, sq1.at[seg], sq1.at[seg], q1_r.at[seg], lax.rem(seg + d, nseg), col)

    from_siblings(None, jb, e_r, 1)
    tail = 1.5 * jb[mine] - 0.5 * product(jb, hcol)

    @pl.when(diag)
    def _():
        out_ref[...] = 1.5 * mb[mine] - 0.5 * tail

    @pl.when(off)
    def _():
        out_ref[...] = -0.5 * tail

    for d in range(1, nseg):
        k = lax.rem(seg + d, nseg)
        arrive(None, sq1.at[k], q1_r.at[k])
    sq2[col] = jnp.sum(sq1[...], axis=0)
    for d in range(1, ncol):
        push(None, sq2.at[col], sq2.at[col], q2_r.at[col], seg, lax.rem(col + d, ncol))
    for d in range(1, ncol):
        k = lax.rem(col + d, ncol)
        arrive(None, sq2.at[k], q2_r.at[k])
    tiles = jnp.sum(sq2[...], axis=0)
    for level in range(2):
        amount = jnp.sum(tiles[8 * level:8 * level + 8], axis=(0, 1), keepdims=True)
        err_ref[level] = jnp.sqrt(amount / order)[0, 0]

    for cond, copy in pending:
        if cond is None:
            copy.wait_send()
        else:
            pl.when(cond)(copy.wait_send)


def body(nseg, ncol, margin, leaf_factor):
    rows, width = leaf_factor.shape
    order = margin.shape[1]
    nx, cq, hc = nseg // 4, ncol // 4, ncol // 2
    dma = pltpu.SemaphoreType.DMA
    factor, errors = pl.pallas_call(
        functools.partial(kernel, nseg, ncol, order),
        out_shape=(
            jax.ShapeDtypeStruct((rows, width), F32),
            jax.ShapeDtypeStruct((2,), F32),
        ),
        in_specs=[pl.BlockSpec(memory_space=pl.ANY), pl.BlockSpec(memory_space=pltpu.VMEM)],
        out_specs=(pl.BlockSpec(memory_space=pltpu.VMEM), pl.BlockSpec(memory_space=pltpu.SMEM)),
        scratch_shapes=[
            pltpu.VMEM((rows, width), F32),
            pltpu.VMEM((nx, rows, width), F32),
            pltpu.VMEM((cq, rows, width), F32),
            pltpu.VMEM((nx, rows, width), F32),
            pltpu.VMEM((nx, rows, width), F32),
            pltpu.VMEM((cq, rows, width), F32),
            pltpu.VMEM((nseg, rows, width), F32),
            pltpu.VMEM((hc, rows, width), F32),
            pltpu.VMEM((hc, rows, width), F32),
            pltpu.VMEM((hc, rows, width), F32),
            pltpu.VMEM((hc, rows, width), F32),
            pltpu.VMEM((hc, rows, width), F32),
            pltpu.VMEM((nseg, 16, 128), F32),
            pltpu.VMEM((ncol, 16, 128), F32),
            dma((SENDS + 16 * nseg,)),
            dma((nx, CHUNKS)),
            dma((cq, CHUNKS)),
            dma((nx, CHUNKS)),
            dma((cq, CHUNKS)),
            dma((4, CHUNKS)),
            dma((nseg, CHUNKS)),
            dma((2, hc)),
            dma((2,)),
            dma((1, hc)),
            dma((2, hc)),
            dma((nseg,)),
            dma((ncol,)),
            dma((1,)),
        ],
        compiler_params=pltpu.CompilerParams(
            collective_id=0, has_side_effects=True, vmem_limit_bytes=56 * 1024 * 1024
        ),
    )(margin, leaf_factor)
    return factor, errors


def solution(mesh):
    return jax.shard_map(
        functools.partial(body, mesh.shape["seg"], mesh.shape["col"]),
        mesh=mesh,
        in_specs=(P("seg", None), P("seg", "col")),
        out_specs=(P("seg", "col"), P()),
        check_vma=False,
    )
```

```python
import functools

import jax
import jax.numpy as jnp
from jax import lax
from jax.experimental import pallas as pl
from jax.experimental.pallas import tpu as pltpu
from jax.sharding import PartitionSpec as P

MESH = pl.DeviceIdType.MESH
F32 = jnp.float32
CHUNKS = 3
RELAYED = 1
SENDS = 192


def dot(left, right, left_dim=1):
    return lax.dot_general(
        left,
        right,
        (((left_dim,), (0,)), ((), ())),
        precision=lax.Precision.HIGHEST,
        preferred_element_type=F32,
    )


def parts(values):
    high = values.astype(jnp.bfloat16)
    return high, (values - high.astype(F32)).astype(jnp.bfloat16)


def dot3(left, right):
    rows = left.shape[0]
    left_high, left_low = parts(left)
    right_high, right_low = parts(right)
    both = jnp.dot(jnp.concatenate([left_high, left_low], axis=0), right_high, preferred_element_type=F32)
    rest = jnp.dot(left_high, right_low, preferred_element_type=F32)
    return both[:rows] + (both[rows:] + rest)


def fold(values):
    rows, width = values.shape
    tall = jnp.sum(values.reshape(rows // 8, 8, width), axis=0)
    total = tall[:, :128]
    for start in range(128, width, 128):
        total = total + tall[:, start:start + 128]
    return total


def kernel(
    nseg, ncol, order,
    margin_ref, leaf_ref, out_ref, err_ref,
    sblk, lcol, lrow, part, rk, ub, kcol, rp, rm, mb, eb, jb, sq1, sq2,
    send, lz_r, lrow_r, rk_r, ub_r, kz_r, kx_r, row_r, pair_r, m_r, e_r, q1_r, q2_r, local,
):
    rows, width = leaf_ref.shape
    nx = nseg // 4
    cq = ncol // 4
    hs, hc = nseg // 2, ncol // 2
    per = width // rows
    quarter = nx * rows
    step = rows // CHUNKS

    seg = lax.axis_index("seg")
    col = lax.axis_index("col")
    z, x = lax.div(seg, nx), lax.rem(seg, nx)
    qc = lax.div(col, cq)
    hseg, hcol = lax.div(z, 2), lax.div(qc, 2)
    diag = hseg == hcol
    mine = lax.rem(col, hc)
    half_col = col - mine

    pending = []
    used = [0]

    def true():
        return seg >= 0

    def push(cond, src, dst, rsem, to_seg, to_col):
        index = used[0]
        used[0] += 1
        copy = pltpu.make_async_remote_copy(
            src_ref=src, dst_ref=dst, send_sem=send.at[index], recv_sem=rsem,
            device_id=(to_seg, to_col), device_id_type=MESH,
        )
        if cond is None:
            copy.start()
        else:
            pl.when(cond)(copy.start)
        pending.append((cond, copy))

    def arrive(cond, dst, rsem):
        copy = pltpu.make_async_remote_copy(
            src_ref=dst, dst_ref=dst, send_sem=send.at[0], recv_sem=rsem,
            device_id=(seg, lax.rem(col + 1, ncol)), device_id_type=MESH,
        )
        if cond is None:
            copy.wait_recv()
        else:
            pl.when(cond)(copy.wait_recv)

    def other_x(d):
        return z * nx + lax.rem(x + d, nx)

    fetch = pltpu.make_async_copy(
        margin_ref.at[:, pl.ds(pl.multiple_of(col * width, 128), width)], sblk, local.at[0]
    )
    fetch.start()
    owner = qc == z
    own_slot = lax.rem(col, cq)

    lcol[...] = jnp.zeros_like(lcol)

    @pl.when(owner)
    def _():
        lcol[x] = leaf_ref[...]
        lrow[own_slot] = leaf_ref[...]

    barrier = pltpu.get_barrier_semaphore()
    for d in range(1, nseg):
        pl.semaphore_signal(barrier, inc=1, device_id=(lax.rem(seg + d, nseg), col), device_id_type=MESH)
    for d in range(1, ncol):
        pl.semaphore_signal(barrier, inc=1, device_id=(seg, lax.rem(col + d, ncol)), device_id_type=MESH)
    pl.semaphore_wait(barrier, nseg + ncol - 2)

    mate = col + 1 - 2 * lax.rem(col, 2)
    for j in range(CHUNKS):
        here = pl.ds(j * step, step)
        for k in range(cq):
            home = z * cq + k
            lead = lax.rem(col, 2) == lax.rem(home, 2)
            block = lrow.at[k, here]
            for d in range(2, ncol, 2):
                push(col == home, block, block, lrow_r.at[k, j], seg, lax.rem(col + d, ncol))
            arrive(lead & (col != home), block, lrow_r.at[k, j])
            push(lead, block, block, lrow_r.at[k, j], seg, mate)
    near = (z - qc <= 1) & (qc - z <= 1)

    def nonzero(slot, j):
        first = slot * rows + j * step
        for place in range(cq):
            start = max(0, first - place * width) // 128 * 128
            if start < width:
                view = lcol.at[slot, pl.ds(j * step, step), pl.ds(start, width - start)]
                yield own_slot == place, view

    def pass_on(chosen):
        for slot in reversed(range(nx)):
            held = chosen & (x >= slot)
            for j in range(CHUNKS):
                sem = lz_r.at[slot, j]
                for placed, block in nonzero(slot, j):
                    use = held & placed
                    arrive(use & jnp.logical_not(owner & (x == slot)), block, sem)
                    push(use & (z >= qc) & (z < 3), block, block, sem, seg + nx, col)
                    push(use & (z <= qc) & (z > 0), block, block, sem, seg - nx, col)
                    for to_x in range(nx):
                        if to_x != slot:
                            cond = use & (x == slot)
                            if to_x > slot:
                                cond = cond & owner
                            push(cond, block, block, sem, z * nx + to_x, col)

    pass_on(near)
    fetch.wait()
    for j in range(CHUNKS):
        for k in range(cq):
            lead = lax.rem(col, 2) == lax.rem(z * cq + k, 2)
            arrive(jnp.logical_not(lead), lrow.at[k, pl.ds(j * step, step)], lrow_r.at[k, j])
    for k in range(cq):
        piece = dot(lrow[k], sblk[...], 0)
        part[pl.ds(k * per, per)] = piece.reshape(per, rows, width)
    for j in range(CHUNKS):
        here = pl.ds(j * step, step)
        for d in range(1, nx):
            to_x = jnp.minimum(x + d, nx - 1)
            push(x + d < nx, part.at[to_x, here], rk.at[x, here], rk_r.at[x, j], z * nx + to_x, col)
    pass_on(jnp.logical_not(near))
    for slot in range(1, nx):
        for j in range(CHUNKS):
            for placed, block in nonzero(slot, j):
                arrive((x < slot) & placed, block, lz_r.at[slot, j])

    def form(j):
        here = pl.ds(j * step, step)
        ub[own_slot, here] = part[x, here]
        for d in range(1, nx):
            from_x = jnp.maximum(x - d, 0)
            arrive(x >= d, rk.at[from_x, here], rk_r.at[from_x, j])

            @pl.when(x >= d)
            def _():
                ub[own_slot, here] += rk[from_x, here]

        first = col - own_slot
        for d in range(1, cq):
            block = ub.at[own_slot, here]
            push(None, block, block, ub_r.at[own_slot, j], seg, first + lax.rem(own_slot + d, cq))
        for d in range(1, cq):
            k = lax.rem(own_slot + d, cq)
            arrive(None, ub.at[k, here], ub_r.at[k, j])
        total = None
        for k in range(cq):
            term = dot(ub[k, here], lcol[pl.ds(k * per, per)].reshape(width, width))
            total = term if total is None else total + term
        kcol[seg, here] = total

    def spread(distance, up, j):
        origin = z - distance if up else z + distance
        valid = (origin >= 0) & (origin <= 3)
        wide = lax.div(origin, 2) == hcol
        same = lax.div(origin, 2) == hseg
        reached = valid & (wide | same)
        low = jnp.where(wide, 0, 2 * hseg)
        high = jnp.where(wide, 3, 2 * hseg + 1)
        plane = jnp.clip(origin, 0, 3)
        slot = plane * nx + x
        block = kcol.at[slot, pl.ds(j * step, step)]
        if distance:
            arrive(reached, block, kz_r.at[plane, j])
        if up or distance == 0:
            push(reached & (z < high), block, block, kz_r.at[plane, j], seg + nx, col)
        if not up or distance == 0:
            push(reached & (z > low), block, block, kz_r.at[plane, j], seg - nx, col)
        across = None if distance == 0 else reached
        if distance == 1 and j < RELAYED:
            across = reached & jnp.logical_not(same)
        for d in range(1, nx):
            push(across, block, block, kx_r.at[slot, j], other_x(d), col)

    def settle(distance, up, j, inside):
        origin = z - distance if up else z + distance
        valid = (origin >= 0) & (origin <= 3)
        same = lax.div(origin, 2) == hseg
        wide = lax.div(origin, 2) == hcol
        reached = valid & (same if inside else wide & jnp.logical_not(same))
        for d in range(1, nx):
            slot = jnp.clip(origin, 0, 3) * nx + lax.rem(x + d, nx)
            arrive(reached, kcol.at[slot, pl.ds(j * step, step)], kx_r.at[slot, j])

    def relay(j):
        sibling = 2 * hseg + 1 - lax.rem(z, 2)
        for d in range(1, nx):
            slot = z * nx + lax.rem(x + d, nx)
            block = kcol.at[slot, pl.ds(j * step, step)]
            arrive(None, block, kx_r.at[slot, j])
            if j < RELAYED:
                push(None, block, block, kx_r.at[slot, j], sibling * nx + x, col)

    for j in range(CHUNKS):
        form(j)
        spread(0, False, j)

    partner = lax.rem(col + hc, ncol)
    row_ids = seg * rows + lax.broadcasted_iota(jnp.int32, (rows, width), 0)
    col_ids = col * width + lax.broadcasted_iota(jnp.int32, (rows, width), 1)
    identity = (row_ids == col_ids).astype(F32)

    def siblings(cond, buf, rsem, which):
        for d in range(1, hc):
            push(cond, buf.at[mine], buf.at[mine], rsem.at[which, mine], seg, half_col + lax.rem(mine + d, hc))

    def from_siblings(cond, buf, rsem, which):
        for d in range(1, hc):
            k = lax.rem(mine + d, hc)
            arrive(cond, buf.at[k], rsem.at[which, k])

    @pl.when(diag)
    def _():
        own = kcol[seg]
        defect = identity - own
        sq1[seg, pl.ds(0, 8)] = fold(defect * defect)
        rp[mine] = 1.5 * identity - 0.5 * own

    @pl.when(jnp.logical_not(diag))
    def _():
        sq1[seg, pl.ds(0, 8)] = jnp.zeros((8, 128), F32)

    push(diag, rp.at[mine], rp.at[mine], pair_r.at[0], seg, partner)
    siblings(diag, rp, row_r, 0)

    off = jnp.logical_not(diag)
    for j in range(CHUNKS):
        spread(1, True, j)
        spread(1, False, j)
    for j in range(CHUNKS):
        relay(j)
        spread(2, True, j)
        spread(2, False, j)
    arrive(off, rp.at[mine], pair_r.at[0])
    siblings(off, rp, row_r, 0)

    @pl.when(diag)
    def _():
        plane = kcol[pl.ds(z * nx, nx)].reshape(quarter, width)
        update = jnp.zeros((rows, width), F32)
        for k in range(cq):
            update = update + dot3(lrow[k], plane[k * width:(k + 1) * width])
        mb[mine] = 1.5 * leaf_ref[...] - 0.5 * update

    siblings(diag, mb, m_r, 0)
    for j in range(CHUNKS):
        settle(1, True, j, True)
        settle(1, False, j, True)
    from_siblings(diag, mb, m_r, 0)

    def product(buf, half):
        total = None
        for k in range(hc):
            term = dot3(buf[k], kcol[pl.ds(half * hs + k * per, per)].reshape(width, width))
            total = term if total is None else total + term
        return total

    @pl.when(diag)
    def _():
        rm[mine] = 1.5 * mb[mine] - 0.5 * product(mb, hseg)

    push(diag, rm.at[mine], rm.at[mine], pair_r.at[1], seg, partner)
    siblings(diag, rm, row_r, 1)

    from_siblings(None, rp, row_r, 0)
    eb[mine] = product(rp, hseg)
    siblings(None, eb, e_r, 0)
    for j in range(CHUNKS):
        spread(3, True, j)
        spread(3, False, j)

    arrive(off, rm.at[mine], pair_r.at[1])
    siblings(off, rm, row_r, 1)
    from_siblings(None, rm, row_r, 1)
    jb[mine] = product(rm, hseg)
    siblings(None, jb, e_r, 1)

    for distance in (1, 2, 3):
        for j in range(CHUNKS):
            settle(distance, True, j, False)
            settle(distance, False, j, False)
    from_siblings(None, eb, e_r, 0)
    coupling = 1.5 * eb[mine] - 0.5 * product(eb, hcol)
    defect = identity - coupling
    sq1[seg, pl.ds(8, 8)] = fold(defect * defect)
    for d in range(1, nseg):
        push(None, sq1.at[seg], sq1.at[seg], q1_r.at[seg], lax.rem(seg + d, nseg), col)

    from_siblings(None, jb, e_r, 1)
    tail = 1.5 * jb[mine] - 0.5 * product(jb, hcol)

    @pl.when(diag)
    def _():
        out_ref[...] = 1.5 * mb[mine] - 0.5 * tail

    @pl.when(off)
    def _():
        out_ref[...] = -0.5 * tail

    for d in range(1, nseg):
        k = lax.rem(seg + d, nseg)
        arrive(None, sq1.at[k], q1_r.at[k])
    sq2[col] = jnp.sum(sq1[...], axis=0)
    for d in range(1, ncol):
        push(None, sq2.at[col], sq2.at[col], q2_r.at[col], seg, lax.rem(col + d, ncol))
    for d in range(1, ncol):
        k = lax.rem(col + d, ncol)
        arrive(None, sq2.at[k], q2_r.at[k])
    tiles = jnp.sum(sq2[...], axis=0)
    for level in range(2):
        amount = jnp.sum(tiles[8 * level:8 * level + 8], axis=(0, 1), keepdims=True)
        err_ref[level] = jnp.sqrt(amount / order)[0, 0]

    for cond, copy in pending:
        if cond is None:
            copy.wait_send()
        else:
            pl.when(cond)(copy.wait_send)


def body(nseg, ncol, margin, leaf_factor):
    rows, width = leaf_factor.shape
    order = margin.shape[1]
    nx, cq, hc = nseg // 4, ncol // 4, ncol // 2
    dma = pltpu.SemaphoreType.DMA
    factor, errors = pl.pallas_call(
        functools.partial(kernel, nseg, ncol, order),
        out_shape=(
            jax.ShapeDtypeStruct((rows, width), F32),
            jax.ShapeDtypeStruct((2,), F32),
        ),
        in_specs=[pl.BlockSpec(memory_space=pl.ANY), pl.BlockSpec(memory_space=pltpu.VMEM)],
        out_specs=(pl.BlockSpec(memory_space=pltpu.VMEM), pl.BlockSpec(memory_space=pltpu.SMEM)),
        scratch_shapes=[
            pltpu.VMEM((rows, width), F32),
            pltpu.VMEM((nx, rows, width), F32),
            pltpu.VMEM((cq, rows, width), F32),
            pltpu.VMEM((nx, rows, width), F32),
            pltpu.VMEM((nx, rows, width), F32),
            pltpu.VMEM((cq, rows, width), F32),
            pltpu.VMEM((nseg, rows, width), F32),
            pltpu.VMEM((hc, rows, width), F32),
            pltpu.VMEM((hc, rows, width), F32),
            pltpu.VMEM((hc, rows, width), F32),
            pltpu.VMEM((hc, rows, width), F32),
            pltpu.VMEM((hc, rows, width), F32),
            pltpu.VMEM((nseg, 16, 128), F32),
            pltpu.VMEM((ncol, 16, 128), F32),
            dma((SENDS + 24 * nseg,)),
            dma((nx, CHUNKS)),
            dma((cq, CHUNKS)),
            dma((nx, CHUNKS)),
            dma((cq, CHUNKS)),
            dma((4, CHUNKS)),
            dma((nseg, CHUNKS)),
            dma((2, hc)),
            dma((2,)),
            dma((1, hc)),
            dma((2, hc)),
            dma((nseg,)),
            dma((ncol,)),
            dma((1,)),
        ],
        compiler_params=pltpu.CompilerParams(
            collective_id=0, has_side_effects=True, vmem_limit_bytes=56 * 1024 * 1024
        ),
    )(margin, leaf_factor)
    return factor, errors


def solution(mesh):
    return jax.shard_map(
        functools.partial(body, mesh.shape["seg"], mesh.shape["col"]),
        mesh=mesh,
        in_specs=(P("seg", None), P("seg", "col")),
        out_specs=(P("seg", "col"), P()),
        check_vma=False,
    )
```

```python
import functools

import jax
import jax.numpy as jnp
from jax import lax
from jax.experimental import pallas as pl
from jax.experimental.pallas import tpu as pltpu
from jax.sharding import PartitionSpec as P

MESH = pl.DeviceIdType.MESH
F32 = jnp.float32
CHUNKS = 3
RELAYED = 1
SENDS = 192


def parts(values):
    high = values.astype(jnp.bfloat16)
    return high, (values - high.astype(F32)).astype(jnp.bfloat16)


def dot3(left, right):
    rows = left.shape[0]
    left_high, left_low = parts(left)
    right_high, right_low = parts(right)
    both = jnp.dot(jnp.concatenate([left_high, left_low], axis=0), right_high, preferred_element_type=F32)
    rest = jnp.dot(left_high, right_low, preferred_element_type=F32)
    return both[:rows] + (both[rows:] + rest)


def fold(values):
    rows, width = values.shape
    tall = jnp.sum(values.reshape(rows // 8, 8, width), axis=0)
    total = tall[:, :128]
    for start in range(128, width, 128):
        total = total + tall[:, start:start + 128]
    return total


def kernel(
    nseg, ncol, order,
    margin_ref, leaf_hbm, out_ref, err_ref,
    leaf_ref, sblk, lcol, lrow, part, rk, ub, kcol, rp, rm, mb, eb, jb, sq1, sq2,
    send, lz_r, lrow_r, rk_r, ub_r, kz_r, kx_r, row_r, pair_r, m_r, e_r, q1_r, q2_r, local,
):
    rows, width = leaf_hbm.shape
    nx = nseg // 4
    cq = ncol // 4
    hs, hc = nseg // 2, ncol // 2
    per = width // rows
    quarter = nx * rows
    step = rows // CHUNKS

    seg = lax.axis_index("seg")
    col = lax.axis_index("col")
    z, x = lax.div(seg, nx), lax.rem(seg, nx)
    qc = lax.div(col, cq)
    hseg, hcol = lax.div(z, 2), lax.div(qc, 2)
    diag = hseg == hcol
    mine = lax.rem(col, hc)
    half_col = col - mine

    pending = []
    used = [0]

    def true():
        return seg >= 0

    def push(cond, src, dst, rsem, to_seg, to_col):
        index = used[0]
        used[0] += 1
        copy = pltpu.make_async_remote_copy(
            src_ref=src, dst_ref=dst, send_sem=send.at[index], recv_sem=rsem,
            device_id=(to_seg, to_col), device_id_type=MESH,
        )
        if cond is None:
            copy.start()
        else:
            pl.when(cond)(copy.start)
        pending.append((cond, copy))

    def arrive(cond, dst, rsem):
        copy = pltpu.make_async_remote_copy(
            src_ref=dst, dst_ref=dst, send_sem=send.at[0], recv_sem=rsem,
            device_id=(seg, lax.rem(col + 1, ncol)), device_id_type=MESH,
        )
        if cond is None:
            copy.wait_recv()
        else:
            pl.when(cond)(copy.wait_recv)

    def other_x(d):
        return z * nx + lax.rem(x + d, nx)

    fetch = pltpu.make_async_copy(
        margin_ref.at[:, pl.ds(pl.multiple_of(col * width, 128), width)], sblk, local.at[0]
    )
    fetch.start()
    owner = qc == z
    own_slot = lax.rem(col, cq)

    lcol[...] = jnp.zeros_like(lcol)
    barrier = pltpu.get_barrier_semaphore()
    for d in range(1, nseg):
        pl.semaphore_signal(barrier, inc=1, device_id=(lax.rem(seg + d, nseg), col), device_id_type=MESH)
    for d in range(1, ncol):
        pl.semaphore_signal(barrier, inc=1, device_id=(seg, lax.rem(col + d, ncol)), device_id_type=MESH)
    load = pltpu.make_async_copy(leaf_hbm, leaf_ref, local.at[1])
    load.start()
    load.wait()

    @pl.when(owner)
    def _():
        lrow[own_slot] = leaf_ref[...]
        lcol[x] = leaf_ref[...]

    pl.semaphore_wait(barrier, nseg + ncol - 2)

    mate = col + 1 - 2 * lax.rem(col, 2)
    for j in range(CHUNKS):
        here = pl.ds(j * step, step)
        for k in range(cq):
            home = z * cq + k
            lead = lax.rem(col, 2) == lax.rem(home, 2)
            block = lrow.at[k, here]
            for d in range(2, ncol, 2):
                push(col == home, block, block, lrow_r.at[k, j], seg, lax.rem(col + d, ncol))
            arrive(lead & (col != home), block, lrow_r.at[k, j])
            push(lead, block, block, lrow_r.at[k, j], seg, mate)
    near = (z - qc <= 1) & (qc - z <= 1)

    def nonzero(slot, j):
        first = slot * rows + j * step
        for place in range(cq):
            start = max(0, first - place * width) // 128 * 128
            if start < width:
                view = lcol.at[slot, pl.ds(j * step, step), pl.ds(start, width - start)]
                yield own_slot == place, view

    def pass_on(chosen):
        for slot in reversed(range(nx)):
            held = chosen & (x >= slot)
            for j in range(CHUNKS):
                sem = lz_r.at[slot, j]
                for placed, block in nonzero(slot, j):
                    use = held & placed
                    arrive(use & jnp.logical_not(owner & (x == slot)), block, sem)
                    push(use & (z >= qc) & (z < 3), block, block, sem, seg + nx, col)
                    push(use & (z <= qc) & (z > 0), block, block, sem, seg - nx, col)
                    for to_x in range(nx):
                        if to_x != slot:
                            cond = use & (x == slot)
                            if to_x > slot:
                                cond = cond & owner
                            push(cond, block, block, sem, z * nx + to_x, col)

    pass_on(near)
    fetch.wait()
    for j in range(CHUNKS):
        for k in range(cq):
            lead = lax.rem(col, 2) == lax.rem(z * cq + k, 2)
            arrive(jnp.logical_not(lead), lrow.at[k, pl.ds(j * step, step)], lrow_r.at[k, j])
    for k in range(cq):
        piece = dot3(lrow[k].T, sblk[...])
        part[pl.ds(k * per, per)] = piece.reshape(per, rows, width)
    for j in range(CHUNKS):
        here = pl.ds(j * step, step)
        for d in range(1, nx):
            to_x = jnp.minimum(x + d, nx - 1)
            push(x + d < nx, part.at[to_x, here], rk.at[x, here], rk_r.at[x, j], z * nx + to_x, col)
    pass_on(jnp.logical_not(near))
    for slot in range(1, nx):
        for j in range(CHUNKS):
            for placed, block in nonzero(slot, j):
                arrive((x < slot) & placed, block, lz_r.at[slot, j])

    def form(j):
        here = pl.ds(j * step, step)
        ub[own_slot, here] = part[x, here]
        for d in range(1, nx):
            from_x = jnp.maximum(x - d, 0)
            arrive(x >= d, rk.at[from_x, here], rk_r.at[from_x, j])

            @pl.when(x >= d)
            def _():
                ub[own_slot, here] += rk[from_x, here]

        first = col - own_slot
        for d in range(1, cq):
            block = ub.at[own_slot, here]
            push(None, block, block, ub_r.at[own_slot, j], seg, first + lax.rem(own_slot + d, cq))
        for d in range(1, cq):
            k = lax.rem(own_slot + d, cq)
            arrive(None, ub.at[k, here], ub_r.at[k, j])
        total = None
        for k in range(cq):
            term = dot3(ub[k, here], lcol[pl.ds(k * per, per)].reshape(width, width))
            total = term if total is None else total + term
        kcol[seg, here] = total

    def spread(distance, up, j):
        origin = z - distance if up else z + distance
        valid = (origin >= 0) & (origin <= 3)
        wide = lax.div(origin, 2) == hcol
        same = lax.div(origin, 2) == hseg
        reached = valid & (wide | same)
        low = jnp.where(wide, 0, 2 * hseg)
        high = jnp.where(wide, 3, 2 * hseg + 1)
        plane = jnp.clip(origin, 0, 3)
        slot = plane * nx + x
        block = kcol.at[slot, pl.ds(j * step, step)]
        if distance:
            arrive(reached, block, kz_r.at[plane, j])
        if up or distance == 0:
            push(reached & (z < high), block, block, kz_r.at[plane, j], seg + nx, col)
        if not up or distance == 0:
            push(reached & (z > low), block, block, kz_r.at[plane, j], seg - nx, col)
        across = None if distance == 0 else reached
        if distance == 1 and j < RELAYED:
            across = reached & jnp.logical_not(same)
        for d in range(1, nx):
            push(across, block, block, kx_r.at[slot, j], other_x(d), col)

    def settle(distance, up, j, inside):
        origin = z - distance if up else z + distance
        valid = (origin >= 0) & (origin <= 3)
        same = lax.div(origin, 2) == hseg
        wide = lax.div(origin, 2) == hcol
        reached = valid & (same if inside else wide & jnp.logical_not(same))
        for d in range(1, nx):
            slot = jnp.clip(origin, 0, 3) * nx + lax.rem(x + d, nx)
            arrive(reached, kcol.at[slot, pl.ds(j * step, step)], kx_r.at[slot, j])

    def relay(j):
        sibling = 2 * hseg + 1 - lax.rem(z, 2)
        for d in range(1, nx):
            slot = z * nx + lax.rem(x + d, nx)
            block = kcol.at[slot, pl.ds(j * step, step)]
            arrive(None, block, kx_r.at[slot, j])
            if j < RELAYED:
                push(None, block, block, kx_r.at[slot, j], sibling * nx + x, col)

    for j in range(CHUNKS):
        form(j)
        spread(0, False, j)

    partner = lax.rem(col + hc, ncol)
    row_ids = seg * rows + lax.broadcasted_iota(jnp.int32, (rows, width), 0)
    col_ids = col * width + lax.broadcasted_iota(jnp.int32, (rows, width), 1)
    identity = (row_ids == col_ids).astype(F32)

    def siblings(cond, buf, rsem, which):
        for d in range(1, hc):
            push(cond, buf.at[mine], buf.at[mine], rsem.at[which, mine], seg, half_col + lax.rem(mine + d, hc))

    def from_siblings(cond, buf, rsem, which):
        for d in range(1, hc):
            k = lax.rem(mine + d, hc)
            arrive(cond, buf.at[k], rsem.at[which, k])

    @pl.when(diag)
    def _():
        own = kcol[seg]
        defect = identity - own
        sq1[seg, pl.ds(0, 8)] = fold(defect * defect)
        rp[mine] = 1.5 * identity - 0.5 * own

    @pl.when(jnp.logical_not(diag))
    def _():
        sq1[seg, pl.ds(0, 8)] = jnp.zeros((8, 128), F32)

    push(diag, rp.at[mine], rp.at[mine], pair_r.at[0], seg, partner)
    siblings(diag, rp, row_r, 0)

    off = jnp.logical_not(diag)
    for j in range(CHUNKS):
        spread(1, True, j)
        spread(1, False, j)
    for j in range(CHUNKS):
        relay(j)
        spread(2, True, j)
        spread(2, False, j)
    arrive(off, rp.at[mine], pair_r.at[0])
    siblings(off, rp, row_r, 0)

    @pl.when(diag)
    def _():
        plane = kcol[pl.ds(z * nx, nx)].reshape(quarter, width)
        update = jnp.zeros((rows, width), F32)
        for k in range(cq):
            update = update + dot3(lrow[k], plane[k * width:(k + 1) * width])
        mb[mine] = 1.5 * leaf_ref[...] - 0.5 * update

    siblings(diag, mb, m_r, 0)
    for j in range(CHUNKS):
        settle(1, True, j, True)
        settle(1, False, j, True)
    from_siblings(diag, mb, m_r, 0)

    def product(buf, half):
        left = jnp.concatenate([buf[k] for k in range(hc)], axis=1)
        return dot3(left, kcol[pl.ds(half * hs, hs)].reshape(hs * rows, width))

    @pl.when(diag)
    def _():
        rm[mine] = 1.5 * mb[mine] - 0.5 * product(mb, hseg)

    push(diag, rm.at[mine], rm.at[mine], pair_r.at[1], seg, partner)
    siblings(diag, rm, row_r, 1)

    from_siblings(None, rp, row_r, 0)
    eb[mine] = product(rp, hseg)
    siblings(None, eb, e_r, 0)
    for j in range(CHUNKS):
        spread(3, True, j)
        spread(3, False, j)

    arrive(off, rm.at[mine], pair_r.at[1])
    siblings(off, rm, row_r, 1)
    from_siblings(None, rm, row_r, 1)
    jb[mine] = product(rm, hseg)
    siblings(None, jb, e_r, 1)

    for distance in (1, 2, 3):
        for j in range(CHUNKS):
            settle(distance, True, j, False)
            settle(distance, False, j, False)
    from_siblings(None, eb, e_r, 0)
    coupling = 1.5 * eb[mine] - 0.5 * product(eb, hcol)
    defect = identity - coupling
    sq1[seg, pl.ds(8, 8)] = fold(defect * defect)
    for d in range(1, nseg):
        push(None, sq1.at[seg], sq1.at[seg], q1_r.at[seg], lax.rem(seg + d, nseg), col)

    from_siblings(None, jb, e_r, 1)
    tail = 1.5 * jb[mine] - 0.5 * product(jb, hcol)

    @pl.when(diag)
    def _():
        out_ref[...] = 1.5 * mb[mine] - 0.5 * tail

    @pl.when(off)
    def _():
        out_ref[...] = -0.5 * tail

    for d in range(1, nseg):
        k = lax.rem(seg + d, nseg)
        arrive(None, sq1.at[k], q1_r.at[k])
    sq2[col] = jnp.sum(sq1[...], axis=0)
    for d in range(1, ncol):
        push(None, sq2.at[col], sq2.at[col], q2_r.at[col], seg, lax.rem(col + d, ncol))
    for d in range(1, ncol):
        k = lax.rem(col + d, ncol)
        arrive(None, sq2.at[k], q2_r.at[k])
    tiles = jnp.sum(sq2[...], axis=0)
    for level in range(2):
        amount = jnp.sum(tiles[8 * level:8 * level + 8], axis=(0, 1), keepdims=True)
        err_ref[level] = jnp.sqrt(amount / order)[0, 0]

    for cond, copy in pending:
        if cond is None:
            copy.wait_send()
        else:
            pl.when(cond)(copy.wait_send)


def body(nseg, ncol, margin, leaf_factor):
    rows, width = leaf_factor.shape
    order = margin.shape[1]
    nx, cq, hc = nseg // 4, ncol // 4, ncol // 2
    dma = pltpu.SemaphoreType.DMA
    factor, errors = pl.pallas_call(
        functools.partial(kernel, nseg, ncol, order),
        out_shape=(
            jax.ShapeDtypeStruct((rows, width), F32),
            jax.ShapeDtypeStruct((2,), F32),
        ),
        in_specs=[pl.BlockSpec(memory_space=pl.ANY)] * 2,
        out_specs=(pl.BlockSpec(memory_space=pltpu.VMEM), pl.BlockSpec(memory_space=pltpu.SMEM)),
        scratch_shapes=[
            pltpu.VMEM((rows, width), F32),
            pltpu.VMEM((rows, width), F32),
            pltpu.VMEM((nx, rows, width), F32),
            pltpu.VMEM((cq, rows, width), F32),
            pltpu.VMEM((nx, rows, width), F32),
            pltpu.VMEM((nx, rows, width), F32),
            pltpu.VMEM((cq, rows, width), F32),
            pltpu.VMEM((nseg, rows, width), F32),
            pltpu.VMEM((hc, rows, width), F32),
            pltpu.VMEM((hc, rows, width), F32),
            pltpu.VMEM((hc, rows, width), F32),
            pltpu.VMEM((hc, rows, width), F32),
            pltpu.VMEM((hc, rows, width), F32),
            pltpu.VMEM((nseg, 16, 128), F32),
            pltpu.VMEM((ncol, 16, 128), F32),
            dma((SENDS + 24 * nseg,)),
            dma((nx, CHUNKS)),
            dma((cq, CHUNKS)),
            dma((nx, CHUNKS)),
            dma((cq, CHUNKS)),
            dma((4, CHUNKS)),
            dma((nseg, CHUNKS)),
            dma((2, hc)),
            dma((2,)),
            dma((1, hc)),
            dma((2, hc)),
            dma((nseg,)),
            dma((ncol,)),
            dma((2,)),
        ],
        compiler_params=pltpu.CompilerParams(
            collective_id=0, has_side_effects=True, vmem_limit_bytes=56 * 1024 * 1024
        ),
    )(margin, leaf_factor)
    return factor, errors


def solution(mesh):
    return jax.shard_map(
        functools.partial(body, mesh.shape["seg"], mesh.shape["col"]),
        mesh=mesh,
        in_specs=(P("seg", None), P("seg", "col")),
        out_specs=(P("seg", "col"), P()),
        check_vma=False,
    )
```

```python
import functools

import jax
import jax.numpy as jnp
from jax import lax
from jax.experimental import pallas as pl
from jax.experimental.pallas import tpu as pltpu
from jax.sharding import PartitionSpec as P

MESH = pl.DeviceIdType.MESH
F32 = jnp.float32
CHUNKS = 3
PIECES = 6
RELAYED = 2
SENDS = 256


def parts(values):
    high = values.astype(jnp.bfloat16)
    return high, (values - high.astype(F32)).astype(jnp.bfloat16)


def dot3(left, right):
    rows = left.shape[0]
    left_high, left_low = parts(left)
    right_high, right_low = parts(right)
    both = jnp.dot(jnp.concatenate([left_high, left_low], axis=0), right_high, preferred_element_type=F32)
    rest = jnp.dot(left_high, right_low, preferred_element_type=F32)
    return both[:rows] + (both[rows:] + rest)


def fold(values):
    rows, width = values.shape
    tall = jnp.sum(values.reshape(rows // 8, 8, width), axis=0)
    total = tall[:, :128]
    for start in range(128, width, 128):
        total = total + tall[:, start:start + 128]
    return total


def kernel(
    nseg, ncol, order,
    margin_ref, leaf_hbm, out_ref, err_ref,
    leaf_ref, sblk, lcol, lrow, part, rk, ub, kcol, rp, rm, mb, eb, jb, sq1, sq2,
    send, lz_r, lrow_r, rk_r, ub_r, kz_r, kx_r, row_r, pair_r, m_r, e_r, q1_r, q2_r, local,
):
    rows, width = leaf_hbm.shape
    nx = nseg // 4
    cq = ncol // 4
    hs, hc = nseg // 2, ncol // 2
    per = width // rows
    quarter = nx * rows
    step = rows // CHUNKS
    size = rows // PIECES

    seg = lax.axis_index("seg")
    col = lax.axis_index("col")
    z, x = lax.div(seg, nx), lax.rem(seg, nx)
    qc = lax.div(col, cq)
    hseg, hcol = lax.div(z, 2), lax.div(qc, 2)
    diag = hseg == hcol
    mine = lax.rem(col, hc)
    half_col = col - mine

    pending = []
    used = [0]

    def true():
        return seg >= 0

    def push(cond, src, dst, rsem, to_seg, to_col):
        index = used[0]
        used[0] += 1
        copy = pltpu.make_async_remote_copy(
            src_ref=src, dst_ref=dst, send_sem=send.at[index], recv_sem=rsem,
            device_id=(to_seg, to_col), device_id_type=MESH,
        )
        if cond is None:
            copy.start()
        else:
            pl.when(cond)(copy.start)
        pending.append((cond, copy))

    def arrive(cond, dst, rsem):
        copy = pltpu.make_async_remote_copy(
            src_ref=dst, dst_ref=dst, send_sem=send.at[0], recv_sem=rsem,
            device_id=(seg, lax.rem(col + 1, ncol)), device_id_type=MESH,
        )
        if cond is None:
            copy.wait_recv()
        else:
            pl.when(cond)(copy.wait_recv)

    def other_x(d):
        return z * nx + lax.rem(x + d, nx)

    fetch = pltpu.make_async_copy(
        margin_ref.at[:, pl.ds(pl.multiple_of(col * width, 128), width)], sblk, local.at[0]
    )
    fetch.start()
    owner = qc == z
    own_slot = lax.rem(col, cq)

    lcol[...] = jnp.zeros_like(lcol)
    barrier = pltpu.get_barrier_semaphore()
    for d in range(1, nseg):
        pl.semaphore_signal(barrier, inc=1, device_id=(lax.rem(seg + d, nseg), col), device_id_type=MESH)
    for d in range(1, ncol):
        pl.semaphore_signal(barrier, inc=1, device_id=(seg, lax.rem(col + d, ncol)), device_id_type=MESH)
    load = pltpu.make_async_copy(leaf_hbm, leaf_ref, local.at[1])
    load.start()
    load.wait()

    @pl.when(owner)
    def _():
        lrow[own_slot] = leaf_ref[...]
        lcol[x] = leaf_ref[...]

    pl.semaphore_wait(barrier, nseg + ncol - 2)

    mate = col + 1 - 2 * lax.rem(col, 2)
    for j in range(CHUNKS):
        here = pl.ds(j * step, step)
        for k in range(cq):
            home = z * cq + k
            lead = lax.rem(col, 2) == lax.rem(home, 2)
            block = lrow.at[k, here]
            for d in range(2, ncol, 2):
                push(col == home, block, block, lrow_r.at[k, j], seg, lax.rem(col + d, ncol))
            arrive(lead & (col != home), block, lrow_r.at[k, j])
            push(lead, block, block, lrow_r.at[k, j], seg, mate)
    near = (z - qc <= 1) & (qc - z <= 1)

    def nonzero(slot, j):
        first = slot * rows + j * step
        for place in range(cq):
            start = max(0, first - place * width) // 128 * 128
            if start < width:
                view = lcol.at[slot, pl.ds(j * step, step), pl.ds(start, width - start)]
                yield own_slot == place, view

    def pass_on(chosen):
        for slot in reversed(range(nx)):
            held = chosen & (x >= slot)
            for j in range(CHUNKS):
                sem = lz_r.at[slot, j]
                for placed, block in nonzero(slot, j):
                    use = held & placed
                    arrive(use & jnp.logical_not(owner & (x == slot)), block, sem)
                    push(use & (z >= qc) & (z < 3), block, block, sem, seg + nx, col)
                    push(use & (z <= qc) & (z > 0), block, block, sem, seg - nx, col)
                    for to_x in range(nx):
                        if to_x != slot:
                            cond = use & (x == slot)
                            if to_x > slot:
                                cond = cond & owner
                            push(cond, block, block, sem, z * nx + to_x, col)

    pass_on(near)
    fetch.wait()
    for j in range(CHUNKS):
        for k in range(cq):
            lead = lax.rem(col, 2) == lax.rem(z * cq + k, 2)
            arrive(jnp.logical_not(lead), lrow.at[k, pl.ds(j * step, step)], lrow_r.at[k, j])
    for k in range(cq):
        piece = dot3(lrow[k].T, sblk[...])
        part[pl.ds(k * per, per)] = piece.reshape(per, rows, width)
    for j in range(CHUNKS):
        here = pl.ds(j * step, step)
        for d in range(1, nx):
            to_x = jnp.minimum(x + d, nx - 1)
            push(x + d < nx, part.at[to_x, here], rk.at[x, here], rk_r.at[x, j], z * nx + to_x, col)
    pass_on(jnp.logical_not(near))
    for slot in range(1, nx):
        for j in range(CHUNKS):
            for placed, block in nonzero(slot, j):
                arrive((x < slot) & placed, block, lz_r.at[slot, j])

    def form(j):
        here = pl.ds(j * step, step)
        ub[own_slot, here] = part[x, here]
        for d in range(1, nx):
            from_x = jnp.maximum(x - d, 0)
            arrive(x >= d, rk.at[from_x, here], rk_r.at[from_x, j])

            @pl.when(x >= d)
            def _():
                ub[own_slot, here] += rk[from_x, here]

        first = col - own_slot
        for d in range(1, cq):
            block = ub.at[own_slot, here]
            push(None, block, block, ub_r.at[own_slot, j], seg, first + lax.rem(own_slot + d, cq))
        for d in range(1, cq):
            k = lax.rem(own_slot + d, cq)
            arrive(None, ub.at[k, here], ub_r.at[k, j])
        total = None
        for k in range(cq):
            term = dot3(ub[k, here], lcol[pl.ds(k * per, per)].reshape(width, width))
            total = term if total is None else total + term
        kcol[seg, here] = total

    def spread(distance, up, j):
        origin = z - distance if up else z + distance
        valid = (origin >= 0) & (origin <= 3)
        wide = lax.div(origin, 2) == hcol
        same = lax.div(origin, 2) == hseg
        reached = valid & (wide | same)
        low = jnp.where(wide, 0, 2 * hseg)
        high = jnp.where(wide, 3, 2 * hseg + 1)
        plane = jnp.clip(origin, 0, 3)
        slot = plane * nx + x
        block = kcol.at[slot, pl.ds(j * size, size)]
        if distance:
            arrive(reached, block, kz_r.at[plane, j])
        if distance < 3 and (up or distance == 0):
            push(reached & (z < high), block, block, kz_r.at[plane, j], seg + nx, col)
        if distance < 3 and not up:
            push(reached & (z > low), block, block, kz_r.at[plane, j], seg - nx, col)
        across = None if distance == 0 else reached
        if distance == 1 and j < RELAYED:
            across = reached & jnp.logical_not(same)
        for d in range(1, nx):
            push(across, block, block, kx_r.at[slot, j], other_x(d), col)

    def settle(distance, up, j, inside):
        origin = z - distance if up else z + distance
        valid = (origin >= 0) & (origin <= 3)
        same = lax.div(origin, 2) == hseg
        wide = lax.div(origin, 2) == hcol
        reached = valid & (same if inside else wide & jnp.logical_not(same))
        for d in range(1, nx):
            slot = jnp.clip(origin, 0, 3) * nx + lax.rem(x + d, nx)
            arrive(reached, kcol.at[slot, pl.ds(j * size, size)], kx_r.at[slot, j])

    def relay(j):
        sibling = 2 * hseg + 1 - lax.rem(z, 2)
        for d in range(1, nx):
            slot = z * nx + lax.rem(x + d, nx)
            block = kcol.at[slot, pl.ds(j * size, size)]
            arrive(None, block, kx_r.at[slot, j])
            if j < RELAYED:
                push(None, block, block, kx_r.at[slot, j], sibling * nx + x, col)

    for j in range(CHUNKS):
        form(j)
        for piece in range(j * PIECES // CHUNKS, (j + 1) * PIECES // CHUNKS):
            spread(0, False, piece)

    partner = lax.rem(col + hc, ncol)
    row_ids = seg * rows + lax.broadcasted_iota(jnp.int32, (rows, width), 0)
    col_ids = col * width + lax.broadcasted_iota(jnp.int32, (rows, width), 1)
    identity = (row_ids == col_ids).astype(F32)

    def siblings(cond, buf, rsem, which):
        for d in range(1, hc):
            push(cond, buf.at[mine], buf.at[mine], rsem.at[which, mine], seg, half_col + lax.rem(mine + d, hc))

    def from_siblings(cond, buf, rsem, which):
        for d in range(1, hc):
            k = lax.rem(mine + d, hc)
            arrive(cond, buf.at[k], rsem.at[which, k])

    @pl.when(diag)
    def _():
        own = kcol[seg]
        defect = identity - own
        sq1[seg, pl.ds(0, 8)] = fold(defect * defect)
        rp[mine] = 1.5 * identity - 0.5 * own

    @pl.when(jnp.logical_not(diag))
    def _():
        sq1[seg, pl.ds(0, 8)] = jnp.zeros((8, 128), F32)

    push(diag, rp.at[mine], rp.at[mine], pair_r.at[0], seg, partner)
    siblings(diag, rp, row_r, 0)

    off = jnp.logical_not(diag)
    for j in range(PIECES):
        spread(1, True, j)
        spread(1, False, j)
    for j in range(PIECES):
        relay(j)
        spread(2, True, j)
        spread(2, False, j)
    arrive(off, rp.at[mine], pair_r.at[0])
    siblings(off, rp, row_r, 0)

    @pl.when(diag)
    def _():
        plane = kcol[pl.ds(z * nx, nx)].reshape(quarter, width)
        update = jnp.zeros((rows, width), F32)
        for k in range(cq):
            update = update + dot3(lrow[k], plane[k * width:(k + 1) * width])
        mb[mine] = 1.5 * leaf_ref[...] - 0.5 * update

    siblings(diag, mb, m_r, 0)
    for j in range(PIECES):
        settle(1, True, j, True)
        settle(1, False, j, True)
    from_siblings(diag, mb, m_r, 0)

    def product(buf, half):
        left = jnp.concatenate([buf[k] for k in range(hc)], axis=1)
        return dot3(left, kcol[pl.ds(half * hs, hs)].reshape(hs * rows, width))

    @pl.when(diag)
    def _():
        rm[mine] = 1.5 * mb[mine] - 0.5 * product(mb, hseg)

    push(diag, rm.at[mine], rm.at[mine], pair_r.at[1], seg, partner)
    siblings(diag, rm, row_r, 1)

    from_siblings(None, rp, row_r, 0)
    eb[mine] = product(rp, hseg)
    siblings(None, eb, e_r, 0)
    for j in range(PIECES):
        spread(3, True, j)
        spread(3, False, j)

    arrive(off, rm.at[mine], pair_r.at[1])
    siblings(off, rm, row_r, 1)
    from_siblings(None, rm, row_r, 1)
    jb[mine] = product(rm, hseg)
    siblings(None, jb, e_r, 1)

    for distance in (1, 2, 3):
        for j in range(PIECES):
            settle(distance, True, j, False)
            settle(distance, False, j, False)
    from_siblings(None, eb, e_r, 0)
    coupling = 1.5 * eb[mine] - 0.5 * product(eb, hcol)
    defect = identity - coupling
    sq1[seg, pl.ds(8, 8)] = fold(defect * defect)
    for d in range(1, nseg):
        push(None, sq1.at[seg], sq1.at[seg], q1_r.at[seg], lax.rem(seg + d, nseg), col)

    from_siblings(None, jb, e_r, 1)
    tail = 1.5 * jb[mine] - 0.5 * product(jb, hcol)

    @pl.when(diag)
    def _():
        out_ref[...] = 1.5 * mb[mine] - 0.5 * tail

    @pl.when(off)
    def _():
        out_ref[...] = -0.5 * tail

    for d in range(1, nseg):
        k = lax.rem(seg + d, nseg)
        arrive(None, sq1.at[k], q1_r.at[k])
    sq2[col] = jnp.sum(sq1[...], axis=0)
    for d in range(1, ncol):
        push(None, sq2.at[col], sq2.at[col], q2_r.at[col], seg, lax.rem(col + d, ncol))
    for d in range(1, ncol):
        k = lax.rem(col + d, ncol)
        arrive(None, sq2.at[k], q2_r.at[k])
    tiles = jnp.sum(sq2[...], axis=0)
    for level in range(2):
        amount = jnp.sum(tiles[8 * level:8 * level + 8], axis=(0, 1), keepdims=True)
        err_ref[level] = jnp.sqrt(amount / order)[0, 0]

    for cond, copy in pending:
        if cond is None:
            copy.wait_send()
        else:
            pl.when(cond)(copy.wait_send)


def body(nseg, ncol, margin, leaf_factor):
    rows, width = leaf_factor.shape
    order = margin.shape[1]
    nx, cq, hc = nseg // 4, ncol // 4, ncol // 2
    dma = pltpu.SemaphoreType.DMA
    factor, errors = pl.pallas_call(
        functools.partial(kernel, nseg, ncol, order),
        out_shape=(
            jax.ShapeDtypeStruct((rows, width), F32),
            jax.ShapeDtypeStruct((2,), F32),
        ),
        in_specs=[pl.BlockSpec(memory_space=pl.ANY)] * 2,
        out_specs=(pl.BlockSpec(memory_space=pltpu.VMEM), pl.BlockSpec(memory_space=pltpu.SMEM)),
        scratch_shapes=[
            pltpu.VMEM((rows, width), F32),
            pltpu.VMEM((rows, width), F32),
            pltpu.VMEM((nx, rows, width), F32),
            pltpu.VMEM((cq, rows, width), F32),
            pltpu.VMEM((nx, rows, width), F32),
            pltpu.VMEM((nx, rows, width), F32),
            pltpu.VMEM((cq, rows, width), F32),
            pltpu.VMEM((nseg, rows, width), F32),
            pltpu.VMEM((hc, rows, width), F32),
            pltpu.VMEM((hc, rows, width), F32),
            pltpu.VMEM((hc, rows, width), F32),
            pltpu.VMEM((hc, rows, width), F32),
            pltpu.VMEM((hc, rows, width), F32),
            pltpu.VMEM((nseg, 16, 128), F32),
            pltpu.VMEM((ncol, 16, 128), F32),
            dma((SENDS + 32 * nseg,)),
            dma((nx, CHUNKS)),
            dma((cq, CHUNKS)),
            dma((nx, CHUNKS)),
            dma((cq, CHUNKS)),
            dma((4, PIECES)),
            dma((nseg, PIECES)),
            dma((2, hc)),
            dma((2,)),
            dma((1, hc)),
            dma((2, hc)),
            dma((nseg,)),
            dma((ncol,)),
            dma((2,)),
        ],
        compiler_params=pltpu.CompilerParams(
            collective_id=0, has_side_effects=True, vmem_limit_bytes=56 * 1024 * 1024
        ),
    )(margin, leaf_factor)
    return factor, errors


def solution(mesh):
    return jax.shard_map(
        functools.partial(body, mesh.shape["seg"], mesh.shape["col"]),
        mesh=mesh,
        in_specs=(P("seg", None), P("seg", "col")),
        out_specs=(P("seg", "col"), P()),
        check_vma=False,
    )
```

```python
import functools

import jax
import jax.numpy as jnp
from jax import lax
from jax.experimental import pallas as pl
from jax.experimental.pallas import tpu as pltpu
from jax.sharding import PartitionSpec as P

MESH = pl.DeviceIdType.MESH
F32 = jnp.float32
CHUNKS = 2
PIECES = 2
RELAYED = 1
SENDS = 256


def parts(values):
    high = values.astype(jnp.bfloat16)
    return high, (values - high.astype(F32)).astype(jnp.bfloat16)


def dot3(left, right):
    rows = left.shape[0]
    left_high, left_low = parts(left)
    right_high, right_low = parts(right)
    both = jnp.dot(jnp.concatenate([left_high, left_low], axis=0), right_high, preferred_element_type=F32)
    rest = jnp.dot(left_high, right_low, preferred_element_type=F32)
    return both[:rows] + (both[rows:] + rest)


def fold(values):
    rows, width = values.shape
    tall = jnp.sum(values.reshape(rows // 8, 8, width), axis=0)
    total = tall[:, :128]
    for start in range(128, width, 128):
        total = total + tall[:, start:start + 128]
    return total


def kernel(
    nseg, ncol, order,
    margin_ref, leaf_hbm, out_ref, err_ref,
    leaf_ref, sblk, lcol, lrow, part, rk, ub, kcol, rp, rm, mb, eb, jb, sq1, sq2,
    send, lz_r, lrow_r, rk_r, ub_r, kz_r, kx_r, row_r, pair_r, m_r, e_r, q1_r, q2_r, local,
):
    rows, width = leaf_hbm.shape
    nx = nseg // 4
    cq = ncol // 4
    hs, hc = nseg // 2, ncol // 2
    per = width // rows
    quarter = nx * rows
    step = rows // CHUNKS
    size = rows // PIECES

    seg = lax.axis_index("seg")
    col = lax.axis_index("col")
    z, x = lax.div(seg, nx), lax.rem(seg, nx)
    qc = lax.div(col, cq)
    hseg, hcol = lax.div(z, 2), lax.div(qc, 2)
    diag = hseg == hcol
    mine = lax.rem(col, hc)
    half_col = col - mine

    pending = []
    used = [0]

    def true():
        return seg >= 0

    def push(cond, src, dst, rsem, to_seg, to_col):
        index = used[0]
        used[0] += 1
        copy = pltpu.make_async_remote_copy(
            src_ref=src, dst_ref=dst, send_sem=send.at[index], recv_sem=rsem,
            device_id=(to_seg, to_col), device_id_type=MESH,
        )
        if cond is None:
            copy.start()
        else:
            pl.when(cond)(copy.start)
        pending.append((cond, copy))

    def arrive(cond, dst, rsem):
        copy = pltpu.make_async_remote_copy(
            src_ref=dst, dst_ref=dst, send_sem=send.at[0], recv_sem=rsem,
            device_id=(seg, lax.rem(col + 1, ncol)), device_id_type=MESH,
        )
        if cond is None:
            copy.wait_recv()
        else:
            pl.when(cond)(copy.wait_recv)

    def other_x(d):
        return z * nx + lax.rem(x + d, nx)

    fetch = pltpu.make_async_copy(
        margin_ref.at[:, pl.ds(pl.multiple_of(col * width, 128), width)], sblk, local.at[0]
    )
    fetch.start()
    owner = qc == z
    own_slot = lax.rem(col, cq)

    lcol[...] = jnp.zeros_like(lcol)
    barrier = pltpu.get_barrier_semaphore()
    for d in range(1, nseg):
        pl.semaphore_signal(barrier, inc=1, device_id=(lax.rem(seg + d, nseg), col), device_id_type=MESH)
    for d in range(1, ncol):
        pl.semaphore_signal(barrier, inc=1, device_id=(seg, lax.rem(col + d, ncol)), device_id_type=MESH)
    load = pltpu.make_async_copy(leaf_hbm, leaf_ref, local.at[1])
    load.start()
    load.wait()

    @pl.when(owner)
    def _():
        lrow[own_slot] = leaf_ref[...]
        lcol[x] = leaf_ref[...]

    pl.semaphore_wait(barrier, nseg + ncol - 2)

    mate = col + 1 - 2 * lax.rem(col, 2)
    for j in range(CHUNKS):
        here = pl.ds(j * step, step)
        for k in range(cq):
            home = z * cq + k
            lead = lax.rem(col, 2) == lax.rem(home, 2)
            block = lrow.at[k, here]
            for d in range(2, ncol, 2):
                push(col == home, block, block, lrow_r.at[k, j], seg, lax.rem(col + d, ncol))
            arrive(lead & (col != home), block, lrow_r.at[k, j])
            push(lead, block, block, lrow_r.at[k, j], seg, mate)
    near = (z - qc <= 1) & (qc - z <= 1)

    def nonzero(slot, j):
        first = slot * rows + j * step
        for place in range(cq):
            start = max(0, first - place * width) // 128 * 128
            if start < width:
                view = lcol.at[slot, pl.ds(j * step, step), pl.ds(start, width - start)]
                yield own_slot == place, view

    def pass_on(chosen):
        for slot in reversed(range(nx)):
            held = chosen & (x >= slot)
            for j in range(CHUNKS):
                sem = lz_r.at[slot, j]
                for placed, block in nonzero(slot, j):
                    use = held & placed
                    arrive(use & jnp.logical_not(owner & (x == slot)), block, sem)
                    push(use & (z >= qc) & (z < 3), block, block, sem, seg + nx, col)
                    push(use & (z <= qc) & (z > 0), block, block, sem, seg - nx, col)
                    for to_x in range(nx):
                        if to_x != slot:
                            cond = use & (x == slot)
                            if to_x > slot:
                                cond = cond & owner
                            push(cond, block, block, sem, z * nx + to_x, col)

    pass_on(near)
    fetch.wait()
    for j in range(CHUNKS):
        for k in range(cq):
            lead = lax.rem(col, 2) == lax.rem(z * cq + k, 2)
            arrive(jnp.logical_not(lead), lrow.at[k, pl.ds(j * step, step)], lrow_r.at[k, j])
    for k in range(cq):
        piece = dot3(lrow[k].T, sblk[...])
        part[pl.ds(k * per, per)] = piece.reshape(per, rows, width)
    for j in range(CHUNKS):
        here = pl.ds(j * step, step)
        for d in range(1, nx):
            to_x = jnp.minimum(x + d, nx - 1)
            push(x + d < nx, part.at[to_x, here], rk.at[x, here], rk_r.at[x, j], z * nx + to_x, col)
    pass_on(jnp.logical_not(near))
    for slot in range(1, nx):
        for j in range(CHUNKS):
            for placed, block in nonzero(slot, j):
                arrive((x < slot) & placed, block, lz_r.at[slot, j])

    def form(j):
        here = pl.ds(j * step, step)
        ub[own_slot, here] = part[x, here]
        for d in range(1, nx):
            from_x = jnp.maximum(x - d, 0)
            arrive(x >= d, rk.at[from_x, here], rk_r.at[from_x, j])

            @pl.when(x >= d)
            def _():
                ub[own_slot, here] += rk[from_x, here]

        first = col - own_slot
        for d in range(1, cq):
            block = ub.at[own_slot, here]
            push(None, block, block, ub_r.at[own_slot, j], seg, first + lax.rem(own_slot + d, cq))
        for d in range(1, cq):
            k = lax.rem(own_slot + d, cq)
            arrive(None, ub.at[k, here], ub_r.at[k, j])
        total = None
        for k in range(cq):
            term = dot3(ub[k, here], lcol[pl.ds(k * per, per)].reshape(width, width))
            total = term if total is None else total + term
        kcol[seg, here] = total

    def spread(distance, up, j):
        origin = z - distance if up else z + distance
        valid = (origin >= 0) & (origin <= 3)
        wide = lax.div(origin, 2) == hcol
        same = lax.div(origin, 2) == hseg
        reached = valid & (wide | same)
        low = jnp.where(wide, 0, 2 * hseg)
        high = jnp.where(wide, 3, 2 * hseg + 1)
        plane = jnp.clip(origin, 0, 3)
        slot = plane * nx + x
        block = kcol.at[slot, pl.ds(j * size, size)]
        if distance:
            arrive(reached, block, kz_r.at[plane, j])
        if distance < 3 and (up or distance == 0):
            push(reached & (z < high), block, block, kz_r.at[plane, j], seg + nx, col)
        if distance < 3 and not up:
            push(reached & (z > low), block, block, kz_r.at[plane, j], seg - nx, col)
        across = None if distance == 0 else reached
        if distance == 1 and j < RELAYED:
            across = reached & jnp.logical_not(same)
        for d in range(1, nx):
            push(across, block, block, kx_r.at[slot, j], other_x(d), col)

    def settle(distance, up, j, inside):
        origin = z - distance if up else z + distance
        valid = (origin >= 0) & (origin <= 3)
        same = lax.div(origin, 2) == hseg
        wide = lax.div(origin, 2) == hcol
        reached = valid & (same if inside else wide & jnp.logical_not(same))
        for d in range(1, nx):
            slot = jnp.clip(origin, 0, 3) * nx + lax.rem(x + d, nx)
            arrive(reached, kcol.at[slot, pl.ds(j * size, size)], kx_r.at[slot, j])

    def relay(j):
        sibling = 2 * hseg + 1 - lax.rem(z, 2)
        for d in range(1, nx):
            slot = z * nx + lax.rem(x + d, nx)
            block = kcol.at[slot, pl.ds(j * size, size)]
            arrive(None, block, kx_r.at[slot, j])
            if j < RELAYED:
                push(None, block, block, kx_r.at[slot, j], sibling * nx + x, col)

    for j in range(CHUNKS):
        form(j)
        for piece in range(j * PIECES // CHUNKS, (j + 1) * PIECES // CHUNKS):
            spread(0, False, piece)

    partner = lax.rem(col + hc, ncol)
    row_ids = seg * rows + lax.broadcasted_iota(jnp.int32, (rows, width), 0)
    col_ids = col * width + lax.broadcasted_iota(jnp.int32, (rows, width), 1)
    identity = (row_ids == col_ids).astype(F32)

    def siblings(cond, buf, rsem, which):
        for d in range(1, hc):
            push(cond, buf.at[mine], buf.at[mine], rsem.at[which, mine], seg, half_col + lax.rem(mine + d, hc))

    def from_siblings(cond, buf, rsem, which):
        for d in range(1, hc):
            k = lax.rem(mine + d, hc)
            arrive(cond, buf.at[k], rsem.at[which, k])

    @pl.when(diag)
    def _():
        own = kcol[seg]
        defect = identity - own
        sq1[seg, pl.ds(0, 8)] = fold(defect * defect)
        rp[mine] = 1.5 * identity - 0.5 * own

    @pl.when(jnp.logical_not(diag))
    def _():
        sq1[seg, pl.ds(0, 8)] = jnp.zeros((8, 128), F32)

    push(diag, rp.at[mine], rp.at[mine], pair_r.at[0], seg, partner)
    siblings(diag, rp, row_r, 0)

    off = jnp.logical_not(diag)
    for j in range(PIECES):
        spread(1, True, j)
        spread(1, False, j)
    for j in range(PIECES):
        relay(j)
        spread(2, True, j)
        spread(2, False, j)
    arrive(off, rp.at[mine], pair_r.at[0])
    siblings(off, rp, row_r, 0)

    @pl.when(diag)
    def _():
        plane = kcol[pl.ds(z * nx, nx)].reshape(quarter, width)
        update = jnp.zeros((rows, width), F32)
        for k in range(cq):
            update = update + dot3(lrow[k], plane[k * width:(k + 1) * width])
        mb[mine] = 1.5 * leaf_ref[...] - 0.5 * update

    siblings(diag, mb, m_r, 0)
    for j in range(PIECES):
        settle(1, True, j, True)
        settle(1, False, j, True)
    from_siblings(diag, mb, m_r, 0)

    def product(buf, half):
        left = jnp.concatenate([buf[k] for k in range(hc)], axis=1)
        return dot3(left, kcol[pl.ds(half * hs, hs)].reshape(hs * rows, width))

    @pl.when(diag)
    def _():
        rm[mine] = 1.5 * mb[mine] - 0.5 * product(mb, hseg)

    push(diag, rm.at[mine], rm.at[mine], pair_r.at[1], seg, partner)
    siblings(diag, rm, row_r, 1)

    from_siblings(None, rp, row_r, 0)
    eb[mine] = product(rp, hseg)
    siblings(None, eb, e_r, 0)
    for j in range(PIECES):
        spread(3, True, j)
        spread(3, False, j)

    arrive(off, rm.at[mine], pair_r.at[1])
    siblings(off, rm, row_r, 1)
    from_siblings(None, rm, row_r, 1)
    jb[mine] = product(rm, hseg)
    siblings(None, jb, e_r, 1)

    for distance in (1, 2, 3):
        for j in range(PIECES):
            settle(distance, True, j, False)
            settle(distance, False, j, False)
    from_siblings(None, eb, e_r, 0)
    coupling = 1.5 * eb[mine] - 0.5 * product(eb, hcol)
    defect = identity - coupling
    sq1[seg, pl.ds(8, 8)] = fold(defect * defect)
    for d in range(1, nseg):
        push(None, sq1.at[seg], sq1.at[seg], q1_r.at[seg], lax.rem(seg + d, nseg), col)

    from_siblings(None, jb, e_r, 1)
    tail = 1.5 * jb[mine] - 0.5 * product(jb, hcol)

    @pl.when(diag)
    def _():
        out_ref[...] = 1.5 * mb[mine] - 0.5 * tail

    @pl.when(off)
    def _():
        out_ref[...] = -0.5 * tail

    for d in range(1, nseg):
        k = lax.rem(seg + d, nseg)
        arrive(None, sq1.at[k], q1_r.at[k])
    sq2[col] = jnp.sum(sq1[...], axis=0)
    for d in range(1, ncol):
        push(None, sq2.at[col], sq2.at[col], q2_r.at[col], seg, lax.rem(col + d, ncol))
    for d in range(1, ncol):
        k = lax.rem(col + d, ncol)
        arrive(None, sq2.at[k], q2_r.at[k])
    tiles = jnp.sum(sq2[...], axis=0)
    for level in range(2):
        amount = jnp.sum(tiles[8 * level:8 * level + 8], axis=(0, 1), keepdims=True)
        err_ref[level] = jnp.sqrt(amount / order)[0, 0]

    for cond, copy in pending:
        if cond is None:
            copy.wait_send()
        else:
            pl.when(cond)(copy.wait_send)


def hand_on(factor_in, err_in, factor_out, err_out, sem):
    copy = pltpu.make_async_copy(factor_in, factor_out, sem)
    copy.start()
    for level in range(2):
        err_out[level] = err_in[level]
    copy.wait()


def body(nseg, ncol, margin, leaf_factor):
    rows, width = leaf_factor.shape
    order = margin.shape[1]
    nx, cq, hc = nseg // 4, ncol // 4, ncol // 2
    dma = pltpu.SemaphoreType.DMA
    factor, errors = pl.pallas_call(
        functools.partial(kernel, nseg, ncol, order),
        out_shape=(
            jax.ShapeDtypeStruct((rows, width), F32),
            jax.ShapeDtypeStruct((2,), F32),
        ),
        in_specs=[pl.BlockSpec(memory_space=pl.ANY)] * 2,
        out_specs=(pl.BlockSpec(memory_space=pltpu.VMEM), pl.BlockSpec(memory_space=pltpu.SMEM)),
        scratch_shapes=[
            pltpu.VMEM((rows, width), F32),
            pltpu.VMEM((rows, width), F32),
            pltpu.VMEM((nx, rows, width), F32),
            pltpu.VMEM((cq, rows, width), F32),
            pltpu.VMEM((nx, rows, width), F32),
            pltpu.VMEM((nx, rows, width), F32),
            pltpu.VMEM((cq, rows, width), F32),
            pltpu.VMEM((nseg, rows, width), F32),
            pltpu.VMEM((hc, rows, width), F32),
            pltpu.VMEM((hc, rows, width), F32),
            pltpu.VMEM((hc, rows, width), F32),
            pltpu.VMEM((hc, rows, width), F32),
            pltpu.VMEM((hc, rows, width), F32),
            pltpu.VMEM((nseg, 16, 128), F32),
            pltpu.VMEM((ncol, 16, 128), F32),
            dma((SENDS + 32 * nseg,)),
            dma((nx, CHUNKS)),
            dma((cq, CHUNKS)),
            dma((nx, CHUNKS)),
            dma((cq, CHUNKS)),
            dma((4, PIECES)),
            dma((nseg, PIECES)),
            dma((2, hc)),
            dma((2,)),
            dma((1, hc)),
            dma((2, hc)),
            dma((nseg,)),
            dma((ncol,)),
            dma((2,)),
        ],
        compiler_params=pltpu.CompilerParams(
            collective_id=0, has_side_effects=True, vmem_limit_bytes=56 * 1024 * 1024
        ),
    )(margin, leaf_factor)
    return pl.pallas_call(
        hand_on,
        out_shape=(jax.ShapeDtypeStruct((rows, width), F32), jax.ShapeDtypeStruct((2,), F32)),
        in_specs=[pl.BlockSpec(memory_space=pl.ANY), pl.BlockSpec(memory_space=pltpu.SMEM)],
        out_specs=(pl.BlockSpec(memory_space=pl.ANY), pl.BlockSpec(memory_space=pltpu.SMEM)),
        scratch_shapes=[pltpu.SemaphoreType.DMA],
    )(factor, errors)


def solution(mesh):
    return jax.shard_map(
        functools.partial(body, mesh.shape["seg"], mesh.shape["col"]),
        mesh=mesh,
        in_specs=(P("seg", None), P("seg", "col")),
        out_specs=(P("seg", "col"), P()),
        check_vma=False,
    )
```

```python
import functools

import jax
import jax.numpy as jnp
from jax import lax
from jax.experimental import pallas as pl
from jax.experimental.pallas import tpu as pltpu
from jax.sharding import PartitionSpec as P

MESH = pl.DeviceIdType.MESH
F32 = jnp.float32
CHUNKS = 3
PIECES = 3
RELAYED = 0
SENDS = 256


def parts(values):
    high = values.astype(jnp.bfloat16)
    return high, (values - high.astype(F32)).astype(jnp.bfloat16)


def dot3(left, right):
    rows = left.shape[0]
    left_high, left_low = parts(left)
    right_high, right_low = parts(right)
    both = jnp.dot(jnp.concatenate([left_high, left_low], axis=0), right_high, preferred_element_type=F32)
    rest = jnp.dot(left_high, right_low, preferred_element_type=F32)
    return both[:rows] + (both[rows:] + rest)


def fold(values):
    rows, width = values.shape
    tall = jnp.sum(values.reshape(rows // 8, 8, width), axis=0)
    total = tall[:, :128]
    for start in range(128, width, 128):
        total = total + tall[:, start:start + 128]
    return total


def kernel(
    nseg, ncol, order,
    margin_ref, leaf_hbm, out_ref, err_ref,
    leaf_ref, sblk, lcol, lrow, part, rk, ub, kcol, rp, rm, mb, eb, jb, sq1, sq2,
    send, lz_r, lrow_r, rk_r, ub_r, kz_r, kx_r, row_r, pair_r, m_r, e_r, q1_r, q2_r, local,
):
    rows, width = leaf_hbm.shape
    nx = nseg // 4
    cq = ncol // 4
    hs, hc = nseg // 2, ncol // 2
    per = width // rows
    quarter = nx * rows
    step = rows // CHUNKS
    size = rows // PIECES

    seg = lax.axis_index("seg")
    col = lax.axis_index("col")
    z, x = lax.div(seg, nx), lax.rem(seg, nx)
    qc = lax.div(col, cq)
    hseg, hcol = lax.div(z, 2), lax.div(qc, 2)
    diag = hseg == hcol
    mine = lax.rem(col, hc)
    half_col = col - mine

    pending = []
    used = [0]

    def true():
        return seg >= 0

    def push(cond, src, dst, rsem, to_seg, to_col):
        index = used[0]
        used[0] += 1
        copy = pltpu.make_async_remote_copy(
            src_ref=src, dst_ref=dst, send_sem=send.at[index], recv_sem=rsem,
            device_id=(to_seg, to_col), device_id_type=MESH,
        )
        if cond is None:
            copy.start()
        else:
            pl.when(cond)(copy.start)
        pending.append((cond, copy))

    def arrive(cond, dst, rsem):
        copy = pltpu.make_async_remote_copy(
            src_ref=dst, dst_ref=dst, send_sem=send.at[0], recv_sem=rsem,
            device_id=(seg, lax.rem(col + 1, ncol)), device_id_type=MESH,
        )
        if cond is None:
            copy.wait_recv()
        else:
            pl.when(cond)(copy.wait_recv)

    def other_x(d):
        return z * nx + lax.rem(x + d, nx)

    fetch = pltpu.make_async_copy(
        margin_ref.at[:, pl.ds(pl.multiple_of(col * width, 128), width)], sblk, local.at[0]
    )
    fetch.start()
    owner = qc == z
    own_slot = lax.rem(col, cq)

    lcol[...] = jnp.zeros_like(lcol)
    barrier = pltpu.get_barrier_semaphore()
    for d in range(1, nseg):
        pl.semaphore_signal(barrier, inc=1, device_id=(lax.rem(seg + d, nseg), col), device_id_type=MESH)
    for d in range(1, ncol):
        pl.semaphore_signal(barrier, inc=1, device_id=(seg, lax.rem(col + d, ncol)), device_id_type=MESH)
    load = pltpu.make_async_copy(leaf_hbm, leaf_ref, local.at[1])
    load.start()
    load.wait()

    @pl.when(owner)
    def _():
        lrow[own_slot] = leaf_ref[...]
        lcol[x] = leaf_ref[...]

    pl.semaphore_wait(barrier, nseg + ncol - 2)

    mate = col + 1 - 2 * lax.rem(col, 2)
    for j in range(CHUNKS):
        here = pl.ds(j * step, step)
        for k in range(cq):
            home = z * cq + k
            lead = lax.rem(col, 2) == lax.rem(home, 2)
            block = lrow.at[k, here]
            for d in range(2, ncol, 2):
                push(col == home, block, block, lrow_r.at[k, j], seg, lax.rem(col + d, ncol))
            arrive(lead & (col != home), block, lrow_r.at[k, j])
            push(lead, block, block, lrow_r.at[k, j], seg, mate)
    near = (z - qc <= 1) & (qc - z <= 1)

    def nonzero(slot, j):
        first = slot * rows + j * step
        for place in range(cq):
            start = max(0, first - place * width) // 128 * 128
            if start < width:
                view = lcol.at[slot, pl.ds(j * step, step), pl.ds(start, width - start)]
                yield own_slot == place, view

    def pass_on(chosen):
        for slot in reversed(range(nx)):
            held = chosen & (x >= slot)
            for j in range(CHUNKS):
                sem = lz_r.at[slot, j]
                for placed, block in nonzero(slot, j):
                    use = held & placed
                    arrive(use & jnp.logical_not(owner & (x == slot)), block, sem)
                    push(use & (z >= qc) & (z < 3), block, block, sem, seg + nx, col)
                    push(use & (z <= qc) & (z > 0), block, block, sem, seg - nx, col)
                    for to_x in range(nx):
                        if to_x != slot:
                            cond = use & (x == slot)
                            if to_x > slot:
                                cond = cond & owner
                            push(cond, block, block, sem, z * nx + to_x, col)

    pass_on(near)
    fetch.wait()
    for j in range(CHUNKS):
        for k in range(cq):
            lead = lax.rem(col, 2) == lax.rem(z * cq + k, 2)
            arrive(jnp.logical_not(lead), lrow.at[k, pl.ds(j * step, step)], lrow_r.at[k, j])
    for k in range(cq):
        piece = dot3(lrow[k].T, sblk[...])
        part[pl.ds(k * per, per)] = piece.reshape(per, rows, width)
    for j in range(CHUNKS):
        here = pl.ds(j * step, step)
        for d in range(1, nx):
            to_x = jnp.minimum(x + d, nx - 1)
            push(x + d < nx, part.at[to_x, here], rk.at[x, here], rk_r.at[x, j], z * nx + to_x, col)
    pass_on(jnp.logical_not(near))
    for slot in range(1, nx):
        for j in range(CHUNKS):
            for placed, block in nonzero(slot, j):
                arrive((x < slot) & placed, block, lz_r.at[slot, j])

    def form(j):
        here = pl.ds(j * step, step)
        ub[own_slot, here] = part[x, here]
        for d in range(1, nx):
            from_x = jnp.maximum(x - d, 0)
            arrive(x >= d, rk.at[from_x, here], rk_r.at[from_x, j])

            @pl.when(x >= d)
            def _():
                ub[own_slot, here] += rk[from_x, here]

        first = col - own_slot
        for d in range(1, cq):
            block = ub.at[own_slot, here]
            push(None, block, block, ub_r.at[own_slot, j], seg, first + lax.rem(own_slot + d, cq))
        for d in range(1, cq):
            k = lax.rem(own_slot + d, cq)
            arrive(None, ub.at[k, here], ub_r.at[k, j])
        total = None
        for k in range(cq):
            term = dot3(ub[k, here], lcol[pl.ds(k * per, per)].reshape(width, width))
            total = term if total is None else total + term
        kcol[seg, here] = total

    def spread(distance, up, j):
        origin = z - distance if up else z + distance
        valid = (origin >= 0) & (origin <= 3)
        wide = lax.div(origin, 2) == hcol
        same = lax.div(origin, 2) == hseg
        reached = valid & (wide | same)
        low = jnp.where(wide, 0, 2 * hseg)
        high = jnp.where(wide, 3, 2 * hseg + 1)
        plane = jnp.clip(origin, 0, 3)
        slot = plane * nx + x
        block = kcol.at[slot, pl.ds(j * size, size)]
        if distance:
            arrive(reached, block, kz_r.at[plane, j])
        if distance < 3 and (up or distance == 0):
            push(reached & (z < high), block, block, kz_r.at[plane, j], seg + nx, col)
        if distance < 3 and not up:
            push(reached & (z > low), block, block, kz_r.at[plane, j], seg - nx, col)
        across = None if distance == 0 else reached
        if distance == 1 and j < RELAYED:
            across = reached & jnp.logical_not(same)
        for d in range(1, nx):
            push(across, block, block, kx_r.at[slot, j], other_x(d), col)

    def settle(distance, up, j, inside):
        origin = z - distance if up else z + distance
        valid = (origin >= 0) & (origin <= 3)
        same = lax.div(origin, 2) == hseg
        wide = lax.div(origin, 2) == hcol
        reached = valid & (same if inside else wide & jnp.logical_not(same))
        for d in range(1, nx):
            slot = jnp.clip(origin, 0, 3) * nx + lax.rem(x + d, nx)
            arrive(reached, kcol.at[slot, pl.ds(j * size, size)], kx_r.at[slot, j])

    def relay(j):
        sibling = 2 * hseg + 1 - lax.rem(z, 2)
        for d in range(1, nx):
            slot = z * nx + lax.rem(x + d, nx)
            block = kcol.at[slot, pl.ds(j * size, size)]
            arrive(None, block, kx_r.at[slot, j])
            if j < RELAYED:
                push(None, block, block, kx_r.at[slot, j], sibling * nx + x, col)

    for j in range(CHUNKS):
        form(j)
        for piece in range(j * PIECES // CHUNKS, (j + 1) * PIECES // CHUNKS):
            spread(0, False, piece)

    partner = lax.rem(col + hc, ncol)
    row_ids = seg * rows + lax.broadcasted_iota(jnp.int32, (rows, width), 0)
    col_ids = col * width + lax.broadcasted_iota(jnp.int32, (rows, width), 1)
    identity = (row_ids == col_ids).astype(F32)

    def siblings(cond, buf, rsem, which):
        for d in range(1, hc):
            push(cond, buf.at[mine], buf.at[mine], rsem.at[which, mine], seg, half_col + lax.rem(mine + d, hc))

    def from_siblings(cond, buf, rsem, which):
        for d in range(1, hc):
            k = lax.rem(mine + d, hc)
            arrive(cond, buf.at[k], rsem.at[which, k])

    @pl.when(diag)
    def _():
        own = kcol[seg]
        defect = identity - own
        sq1[seg, pl.ds(0, 8)] = fold(defect * defect)
        rp[mine] = 1.5 * identity - 0.5 * own

    @pl.when(jnp.logical_not(diag))
    def _():
        sq1[seg, pl.ds(0, 8)] = jnp.zeros((8, 128), F32)

    push(diag, rp.at[mine], rp.at[mine], pair_r.at[0], seg, partner)
    siblings(diag, rp, row_r, 0)

    off = jnp.logical_not(diag)
    for j in range(PIECES):
        spread(1, True, j)
        spread(1, False, j)
    for j in range(PIECES):
        relay(j)
        spread(2, True, j)
        spread(2, False, j)
    arrive(off, rp.at[mine], pair_r.at[0])
    siblings(off, rp, row_r, 0)

    @pl.when(diag)
    def _():
        plane = kcol[pl.ds(z * nx, nx)].reshape(quarter, width)
        update = jnp.zeros((rows, width), F32)
        for k in range(cq):
            update = update + dot3(lrow[k], plane[k * width:(k + 1) * width])
        mb[mine] = 1.5 * leaf_ref[...] - 0.5 * update

    siblings(diag, mb, m_r, 0)
    for j in range(PIECES):
        settle(1, True, j, True)
        settle(1, False, j, True)
    from_siblings(diag, mb, m_r, 0)

    def product(buf, half):
        left = jnp.concatenate([buf[k] for k in range(hc)], axis=1)
        return dot3(left, kcol[pl.ds(half * hs, hs)].reshape(hs * rows, width))

    @pl.when(diag)
    def _():
        rm[mine] = 1.5 * mb[mine] - 0.5 * product(mb, hseg)

    push(diag, rm.at[mine], rm.at[mine], pair_r.at[1], seg, partner)
    siblings(diag, rm, row_r, 1)

    from_siblings(None, rp, row_r, 0)
    eb[mine] = product(rp, hseg)
    siblings(None, eb, e_r, 0)
    for j in range(PIECES):
        spread(3, True, j)
        spread(3, False, j)

    arrive(off, rm.at[mine], pair_r.at[1])
    siblings(off, rm, row_r, 1)
    from_siblings(None, rm, row_r, 1)
    jb[mine] = product(rm, hseg)
    siblings(None, jb, e_r, 1)

    for distance in (1, 2, 3):
        for j in range(PIECES):
            settle(distance, True, j, False)
            settle(distance, False, j, False)
    from_siblings(None, eb, e_r, 0)
    coupling = 1.5 * eb[mine] - 0.5 * product(eb, hcol)
    defect = identity - coupling
    sq1[seg, pl.ds(8, 8)] = fold(defect * defect)
    for d in range(1, nseg):
        push(None, sq1.at[seg], sq1.at[seg], q1_r.at[seg], lax.rem(seg + d, nseg), col)

    from_siblings(None, jb, e_r, 1)
    tail = 1.5 * jb[mine] - 0.5 * product(jb, hcol)

    @pl.when(diag)
    def _():
        out_ref[...] = 1.5 * mb[mine] - 0.5 * tail

    @pl.when(off)
    def _():
        out_ref[...] = -0.5 * tail

    for d in range(1, nseg):
        k = lax.rem(seg + d, nseg)
        arrive(None, sq1.at[k], q1_r.at[k])
    sq2[col] = jnp.sum(sq1[...], axis=0)
    for d in range(1, ncol):
        push(None, sq2.at[col], sq2.at[col], q2_r.at[col], seg, lax.rem(col + d, ncol))
    for d in range(1, ncol):
        k = lax.rem(col + d, ncol)
        arrive(None, sq2.at[k], q2_r.at[k])
    tiles = jnp.sum(sq2[...], axis=0)
    for level in range(2):
        amount = jnp.sum(tiles[8 * level:8 * level + 8], axis=(0, 1), keepdims=True)
        err_ref[level] = jnp.sqrt(amount / order)[0, 0]

    for cond, copy in pending:
        if cond is None:
            copy.wait_send()
        else:
            pl.when(cond)(copy.wait_send)


def hand_on(factor_in, err_in, factor_out, err_out):
    factor_out[...] = factor_in[...]
    for level in range(2):
        err_out[level] = err_in[level]


def body(nseg, ncol, margin, leaf_factor):
    rows, width = leaf_factor.shape
    order = margin.shape[1]
    nx, cq, hc = nseg // 4, ncol // 4, ncol // 2
    dma = pltpu.SemaphoreType.DMA
    factor, errors = pl.pallas_call(
        functools.partial(kernel, nseg, ncol, order),
        out_shape=(
            jax.ShapeDtypeStruct((rows, width), F32),
            jax.ShapeDtypeStruct((2,), F32),
        ),
        in_specs=[pl.BlockSpec(memory_space=pl.ANY)] * 2,
        out_specs=(pl.BlockSpec(memory_space=pltpu.VMEM), pl.BlockSpec(memory_space=pltpu.SMEM)),
        scratch_shapes=[
            pltpu.VMEM((rows, width), F32),
            pltpu.VMEM((rows, width), F32),
            pltpu.VMEM((nx, rows, width), F32),
            pltpu.VMEM((cq, rows, width), F32),
            pltpu.VMEM((nx, rows, width), F32),
            pltpu.VMEM((nx, rows, width), F32),
            pltpu.VMEM((cq, rows, width), F32),
            pltpu.VMEM((nseg, rows, width), F32),
            pltpu.VMEM((hc, rows, width), F32),
            pltpu.VMEM((hc, rows, width), F32),
            pltpu.VMEM((hc, rows, width), F32),
            pltpu.VMEM((hc, rows, width), F32),
            pltpu.VMEM((hc, rows, width), F32),
            pltpu.VMEM((nseg, 16, 128), F32),
            pltpu.VMEM((ncol, 16, 128), F32),
            dma((SENDS + 32 * nseg,)),
            dma((nx, CHUNKS)),
            dma((cq, CHUNKS)),
            dma((nx, CHUNKS)),
            dma((cq, CHUNKS)),
            dma((4, PIECES)),
            dma((nseg, PIECES)),
            dma((2, hc)),
            dma((2,)),
            dma((1, hc)),
            dma((2, hc)),
            dma((nseg,)),
            dma((ncol,)),
            dma((2,)),
        ],
        compiler_params=pltpu.CompilerParams(
            collective_id=0, has_side_effects=True, vmem_limit_bytes=56 * 1024 * 1024
        ),
    )(margin, leaf_factor)
    return pl.pallas_call(
        hand_on,
        out_shape=(jax.ShapeDtypeStruct((rows, width), F32), jax.ShapeDtypeStruct((2,), F32)),
        in_specs=[pl.BlockSpec(memory_space=pltpu.VMEM), pl.BlockSpec(memory_space=pltpu.SMEM)],
        out_specs=(pl.BlockSpec(memory_space=pltpu.VMEM), pl.BlockSpec(memory_space=pltpu.SMEM)),
    )(factor, errors)


def solution(mesh):
    return jax.shard_map(
        functools.partial(body, mesh.shape["seg"], mesh.shape["col"]),
        mesh=mesh,
        in_specs=(P("seg", None), P("seg", "col")),
        out_specs=(P("seg", "col"), P()),
        check_vma=False,
    )
```
